512 devices in a mesh: section: 16 (over x, y_lo), peer: 32 (over y_hi, z, core).
Axes of the slice: x: 4, y: 8 (y_hi: 2, y_lo: 4; y = y_hi * 4 + y_lo), z: 8, core: 2. Of those that a mesh axis runs over, the one named last changes fastest.
Arguments:
- hidden_in: bfloat16 [32, 128, 4096], P('peer', None, 'section'), may hold values from -6 to 6
- cotangent: bfloat16 [32, 128, 4096], P('peer', None, 'section'), may hold values from -24 to 24
- norm_gain: float32 [16, 4096], P('section'), may hold values from 0.1 to 1.9
- adapter_down: bfloat16 [16, 32, 4096, 32], P('section', 'peer'), may hold values from -6 to 6
- adapter_up: bfloat16 [16, 32, 32, 4096], P('section', 'peer'), may hold values from -6 to 6
- moment_down: bfloat16 [16, 32, 4096, 32], P('section', 'peer'), may hold values from -6 to 6
- moment_up: bfloat16 [16, 32, 32, 4096], P('section', 'peer'), may hold values from -6 to 6
- square_down: bfloat16 [16, 32, 4096, 32], P('section', 'peer'), may hold values from 0.0009994507 to 0.019897461
- square_up: bfloat16 [16, 32, 32, 4096], P('section', 'peer'), may hold values from 0.0009994507 to 0.019897461
- round_bits: int32 [4], replicated, may hold values from 0 to 4, as said below
Outputs:
- peer_down: bfloat16 [16, 32, 4096, 32], P('section', 'peer')
- peer_up: bfloat16 [16, 32, 32, 4096], P('section', 'peer')
- peer_moment_down: bfloat16 [16, 32, 4096, 32], P('section', 'peer')
- peer_moment_up: bfloat16 [16, 32, 32, 4096], P('section', 'peer')
- peer_square_down: bfloat16 [16, 32, 4096, 32], P('section', 'peer')
- peer_square_up: bfloat16 [16, 32, 32, 4096], P('section', 'peer')
The draws below stay inside these ranges and needn't reach their ends.
Inputs may be any that keep to these rules, and one draw needn't show every extreme that they name: `round_bits`: bit 0 and the highest bit are each named by some round; other rounds may name any bit, repeats allowed.
All inputs are finite; a program needn't handle non-finite values.
Results may differ from the reference program's by a relative error of at most 0.03.
Values may be sent and summed in bfloat16 or wider, within the bound.
A program may use at most 64 MiB of HBM per device.

```python
import math
import jax
import jax.numpy as jnp
from jax import lax

DW = 4096
RANK = 32
TOK_PEER = 128
PEER_BITS = 5
ROUNDS = 4
ADAM_STEP = 100
N_SECTION = 16
N_PEER = 32


def draw_round_bits(key, part):
    key = jax.random.fold_in(key, 11)
    extra_key = jax.random.fold_in(key, 3)
    order_key = jax.random.fold_in(key, 5)
    extra = jax.random.randint(extra_key, (ROUNDS - 2,), 0, PEER_BITS).astype(jnp.int32)
    chosen = jnp.concatenate([jnp.zeros((1,), jnp.int32), jnp.full((1,), PEER_BITS - 1, jnp.int32), extra])
    placed = jax.random.permutation(order_key, ROUNDS).astype(jnp.int32)
    return chosen[placed].astype(jnp.int32)


def steps_of(stream_key, extent, split, smallest, largest):
    level = 1.0
    for position, parts in split:
        heights = jax.random.uniform(jax.random.fold_in(jax.random.fold_in(stream_key, 6), position), (parts,), jnp.float32, smallest / len(split), largest / len(split))
        level = level * jnp.repeat(jnp.exp(heights), extent[position] // parts).reshape((-1,) + (1,) * (len(extent) - 1 - position))
    return level


def noise(stream_key, dims, scale, reach, cuts=(), kind=jnp.bfloat16):
    drawn = scale * jax.random.normal(stream_key, dims, jnp.float32)
    if cuts:
        drawn = drawn * steps_of(stream_key, dims, cuts, -0.22, 0.18)
    return jnp.clip(drawn, -reach, reach).astype(kind)


def setup_inputs(seed: int = 0) -> dict:
    key_list = jax.random.split(jax.random.key(seed), 11)
    hidden_in = noise(key_list[0], (N_PEER, TOK_PEER, DW), 1.0, 6.0, ((0, 32), (2, 16)))
    cotangent = noise(key_list[1], (N_PEER, TOK_PEER, DW), 4.0, 24.0, ((0, 32), (2, 16)))
    norm_gain = jnp.clip(1.0 + 0.18 * jax.random.normal(key_list[2], (N_SECTION, DW), jnp.float32), 0.1, 1.9)
    adapter_down = noise(key_list[3], (N_SECTION, N_PEER, DW, RANK), 1.0, 6.0, ((0, 16), (1, 32)))
    adapter_up = noise(key_list[4], (N_SECTION, N_PEER, RANK, DW), 1.0, 6.0, ((0, 16), (1, 32)))
    moment_down = noise(key_list[5], (N_SECTION, N_PEER, DW, RANK), 1.0, 6.0, ((0, 16), (1, 32)))
    moment_up = noise(key_list[6], (N_SECTION, N_PEER, RANK, DW), 1.0, 6.0, ((0, 16), (1, 32)))
    square_down = jnp.clip(jnp.exp(math.log(0.019897461) - 2.9911416 * jax.random.uniform(key_list[7], (N_SECTION, N_PEER, DW, RANK), jnp.float32) ** steps_of(key_list[7], (N_SECTION, N_PEER, DW, RANK), ((0, 16), (1, 32)), -0.2, 0.2)), 0.0009994507, 0.019897461).astype(jnp.bfloat16)
    square_up = jnp.clip(jnp.exp(math.log(0.019897461) - 2.9911416 * jax.random.uniform(key_list[8], (N_SECTION, N_PEER, RANK, DW), jnp.float32) ** steps_of(key_list[8], (N_SECTION, N_PEER, RANK, DW), ((0, 16), (1, 32)), -0.2, 0.2)), 0.0009994507, 0.019897461).astype(jnp.bfloat16)
    round_bits = draw_round_bits(jax.random.fold_in(key_list[10], 71), 0)
    return {"hidden_in": hidden_in, "cotangent": cotangent, "norm_gain": norm_gain, "adapter_down": adapter_down, "adapter_up": adapter_up, "moment_down": moment_down, "moment_up": moment_up, "square_down": square_down, "square_up": square_up, "round_bits": round_bits}


def normalize(hidden, gain):
    values = hidden.astype(jnp.float32)
    scale = lax.rsqrt(lax.optimization_barrier(jnp.mean(values * values, axis=-1, keepdims=True)) + 1e-05)
    normed = (values * scale * gain).astype(jnp.bfloat16)
    return (values, scale, normed)

def layer_forward(hidden, gain, down, upper):
    values, scale, normed = normalize(hidden, gain)
    width = hidden.shape[-1]
    rank = down.shape[-1]
    latent = (jnp.dot(normed, down, preferred_element_type=jnp.float32) * width ** (-0.5)).astype(jnp.bfloat16)
    delta = jnp.dot(latent, upper, preferred_element_type=jnp.float32) * rank ** (-0.5)
    return (values + delta).astype(jnp.bfloat16)

def layer_backward(hidden, grad_out, gain, down, upper):
    values, scale, normed = normalize(hidden, gain)
    width = hidden.shape[-1]
    rank = down.shape[-1]
    latent = (jnp.dot(normed, down, preferred_element_type=jnp.float32) * width ** (-0.5)).astype(jnp.bfloat16)
    grad_up = lax.dot_general(latent, grad_out, (((0,), (0,)), ((), ())), preferred_element_type=jnp.float32) * rank ** (-0.5)
    inner = (lax.dot_general(grad_out, upper, (((1,), (1,)), ((), ())), preferred_element_type=jnp.float32) * rank ** (-0.5)).astype(jnp.bfloat16)
    grad_down = lax.dot_general(normed, inner, (((0,), (0,)), ((), ())), preferred_element_type=jnp.float32) * width ** (-0.5)
    grad_normed = lax.dot_general(inner, down, (((1,), (1,)), ((), ())), preferred_element_type=jnp.float32) * width ** (-0.5)
    weighted = grad_normed * gain
    project = lax.optimization_barrier(jnp.mean(values * weighted, axis=-1, keepdims=True))
    grad_in = scale * weighted - values * scale * scale * scale * project
    return ((grad_out.astype(jnp.float32) + grad_in).astype(jnp.bfloat16), grad_down, grad_up)

def adam_step(param, first, second, grad):
    first_new = 0.9 * first.astype(jnp.float32) + 0.1 * grad
    second_new = 0.999 * second.astype(jnp.float32) + 0.001 * grad * grad
    corr_one = 1.0 - 0.9 ** ADAM_STEP
    corr_two = 1.0 - 0.999 ** ADAM_STEP
    update = 0.05 * (first_new / corr_one) / (jnp.sqrt(second_new / corr_two) + 1e-08)
    return ((param.astype(jnp.float32) - update).astype(jnp.bfloat16), first_new.astype(jnp.bfloat16), second_new.astype(jnp.bfloat16))

def reference(hidden_in, cotangent, norm_gain, adapter_down, adapter_up, moment_down, moment_up, square_down, square_up, round_bits):

    def run_replica(inputs):
        hidden, grad, downs, uppers, first_down, first_up, second_down, second_up = inputs
        stored = []
        for section_number in range(N_SECTION):
            stored.append(hidden)
            hidden = layer_forward(hidden, norm_gain[section_number], downs[section_number], uppers[section_number])
        results = [None] * N_SECTION
        for section_number in reversed(range(N_SECTION)):
            grad, grad_down, grad_up = layer_backward(stored[section_number], grad, norm_gain[section_number], downs[section_number], uppers[section_number])
            new_down, mom_down, sq_down = adam_step(downs[section_number], first_down[section_number], second_down[section_number], grad_down)
            new_up, mom_up, sq_up = adam_step(uppers[section_number], first_up[section_number], second_up[section_number], grad_up)
            results[section_number] = (new_down, new_up, mom_down, mom_up, sq_down, sq_up)
        return tuple((jnp.stack([entry[index] for entry in results]) for index in range(6)))
    moved = tuple((jnp.moveaxis(array, 1, 0) for array in (adapter_down, adapter_up, moment_down, moment_up, square_down, square_up)))
    outputs = lax.map(run_replica, (hidden_in, cotangent) + moved)
    states = [jnp.moveaxis(array, 0, 1) for array in outputs]
    peer_ids = jnp.arange(N_PEER, dtype=jnp.int32)
    for round_number in range(ROUNDS):
        partner = jnp.bitwise_xor(peer_ids, jnp.left_shift(jnp.int32(1), round_bits[round_number]))
        states = [((array.astype(jnp.float32) + jnp.take(array, partner, axis=1).astype(jnp.float32)) * 0.5).astype(jnp.bfloat16) for array in states]
    return (states[0], states[1], states[2], states[3], states[4], states[5])
```

```python
import jax
import jax.numpy as jnp
from jax import lax
from jax.experimental import pallas as pl
from jax.experimental.pallas import tpu as pltpu
from jax.sharding import PartitionSpec as P

ADAM_STEP = 100
MESH = pl.DeviceIdType.MESH
F32, BF16 = jnp.float32, jnp.bfloat16
SECTIONS, NX, NY = 16, 4, 4
RANK, WIDTH, TOKENS = 32, 4096, 128
SLICE = WIDTH // SECTIONS
ALL = SECTIONS * RANK
XW = ALL + 3 * TOKENS
VMEM = pl.BlockSpec(memory_space=pltpu.VMEM)
LIMIT = 48 << 20

NN = (((1,), (0,)), ((), ()))
NT = (((1,), (1,)), ((), ()))


def dot(a, b, dims=NN):
    return lax.dot_general(a, b, dims, preferred_element_type=F32)


def block_masks():
    row = lax.broadcasted_iota(jnp.int32, (ALL, ALL), 0) // RANK
    col = lax.broadcasted_iota(jnp.int32, (ALL, ALL), 1) // RANK
    return row > col, row < col


def remote(src, dst, send, recv, section, peer):
    return pltpu.make_async_remote_copy(
        src_ref=src, dst_ref=dst, send_sem=send, recv_sem=recv, device_id=(section, peer), device_id_type=MESH
    )


def products_kernel(
    h_ref, q_ref, g_ref, a_ref, b_ref, x_ref, n_ref, af_ref, bf_ref,
    scaled, part, rx, px, ry, npart, nrx, npx, nry, sa, ra, sb, rb, sx, rxs, sn, rn, sy, rys, sm, rm, sg, rg, sh, rh,
):
    me, peer = lax.axis_index("section"), lax.axis_index("peer")
    mx, my = me // NY, me % NY

    barrier = pltpu.get_barrier_semaphore()
    for j in range(1, SECTIONS):
        pl.semaphore_signal(barrier, inc=1, device_id=((me + j) % SECTIONS, peer), device_id_type=MESH)
    scaled[...] = (a_ref[...].astype(F32) * (g_ref[...] * WIDTH**-0.5)).astype(BF16)
    pl.semaphore_wait(barrier, SECTIONS - 1)

    mine = pl.ds(pl.multiple_of(me * RANK, RANK), RANK)
    copies = []
    for j in range(1, SECTIONS):
        to = (me + j) % SECTIONS
        cols = pl.ds(pl.multiple_of(to * SLICE, SLICE), SLICE)
        copies.append(remote(scaled.at[:, cols], af_ref.at[mine], sa.at[j], ra.at[j], to, peer))
        copies.append(remote(b_ref.at[:, cols], bf_ref.at[mine], sb.at[j], rb.at[j], to, peer))
    for copy in copies:
        copy.start()
    cols = pl.ds(pl.multiple_of(me * SLICE, SLICE), SLICE)
    af_ref[mine, :] = scaled[:, cols]
    bf_ref[mine, :] = b_ref[:, cols]
    h = h_ref[...]
    square = h.astype(F32) * h.astype(F32)
    high = square.astype(BF16)
    low = (square - high.astype(F32)).astype(BF16)
    ones = jnp.ones((8, SLICE), BF16)
    npart[...] = dot(ones, high, NT) + dot(ones, low, NT)
    for copy in copies:
        copy.wait()

    af, bf = af_ref[...], bf_ref[...]
    rs = RANK**-0.5
    lower, _ = block_masks()
    part[:, 0:ALL] = jnp.where(lower, dot(af, bf, NT) * rs, dot(bf, bf, NT) * (1.0 / RANK)).astype(BF16)
    part[:, ALL : ALL + TOKENS] = dot(af, h, NT).astype(BF16)
    part[:, ALL + TOKENS : ALL + 2 * TOKENS] = (dot(bf, h, NT) * rs).astype(BF16)
    part[:, ALL + 2 * TOKENS : XW] = (dot(bf, q_ref[...], NT) * rs).astype(BF16)

    group = NY * RANK

    def group_rows(x):
        return pl.ds(pl.multiple_of(x * group, group), group)

    copies = []
    for j in range(1, NX):
        x = (mx + j) % NX
        copies.append(remote(part.at[group_rows(x)], rx.at[j - 1], sx.at[j], rxs.at[j], x * NY + my, peer))
        copies.append(remote(npart, nrx.at[j - 1], sn.at[j], rn.at[j], x * NY + my, peer))
    for copy in copies:
        copy.start()
    for copy in copies:
        copy.wait()
    total = part[group_rows(mx), :].astype(F32)
    for j in range(NX - 1):
        total += rx[j].astype(F32)
    px[...] = total.astype(BF16)
    npx[...] = npart[...] + nrx[0] + nrx[1] + nrx[2]

    def rank_rows(y):
        return pl.ds(pl.multiple_of(y * RANK, RANK), RANK)

    copies = []
    for j in range(1, NY):
        y = (my + j) % NY
        copies.append(remote(px.at[rank_rows(y)], ry.at[j - 1], sy.at[j], rys.at[j], mx * NY + y, peer))
        copies.append(remote(npx, nry.at[j - 1], sm.at[j], rm.at[j], mx * NY + y, peer))
    for copy in copies:
        copy.start()
    for copy in copies:
        copy.wait()
    total = px[rank_rows(my), :].astype(F32)
    for j in range(NY - 1):
        total += ry[j].astype(F32)
    x_ref[mine, :] = total.astype(BF16)
    n_ref[...] = npx[...] + nry[0] + nry[1] + nry[2]

    copies = []
    for j in range(1, NY):
        to = mx * NY + (my + j) % NY
        copies.append(remote(x_ref.at[mine], x_ref.at[mine], sg.at[j], rg.at[j], to, peer))
    for copy in copies:
        copy.start()
    for copy in copies:
        copy.wait()
    copies = []
    for j in range(1, NX):
        to = ((mx + j) % NX) * NY + my
        copies.append(remote(x_ref.at[group_rows(mx)], x_ref.at[group_rows(mx)], sh.at[j], rh.at[j], to, peer))
    for copy in copies:
        copy.start()
    for copy in copies:
        copy.wait()


def products(h, q, gain, a, b):
    dma = pltpu.SemaphoreType.DMA
    group = NY * RANK
    return pl.pallas_call(
        products_kernel,
        out_shape=(
            jax.ShapeDtypeStruct((ALL, XW), BF16),
            jax.ShapeDtypeStruct((8, TOKENS), F32),
            jax.ShapeDtypeStruct((ALL, SLICE), BF16),
            jax.ShapeDtypeStruct((ALL, SLICE), BF16),
        ),
        in_specs=[VMEM] * 5,
        out_specs=(VMEM,) * 4,
        scratch_shapes=[
            pltpu.VMEM((RANK, WIDTH), BF16),
            pltpu.VMEM((ALL, XW), BF16),
            pltpu.VMEM((NX - 1, group, XW), BF16),
            pltpu.VMEM((group, XW), BF16),
            pltpu.VMEM((NY - 1, RANK, XW), BF16),
            pltpu.VMEM((8, TOKENS), F32),
            pltpu.VMEM((NX - 1, 8, TOKENS), F32),
            pltpu.VMEM((8, TOKENS), F32),
            pltpu.VMEM((NY - 1, 8, TOKENS), F32),
        ]
        + [dma((SECTIONS,))] * 4
        + [dma((4,))] * 12,
        compiler_params=pltpu.CompilerParams(collective_id=0, has_side_effects=True, vmem_limit_bytes=LIMIT),
        name="products",
    )(h, q, gain, a, b)


def chain_kernel(x_ref, n_ref, af_ref, bf_ref, h_ref, q_ref, gd_ref, gu_ref, xt, lat, scaled_inner, cl, wp, rms):
    rs = RANK**-0.5
    xt[...] = x_ref[:, 0:ALL].astype(F32).T.astype(BF16)

    def rows(s):
        return slice(RANK * s, RANK * s + RANK)

    norm = n_ref[0:1, :]
    for s in range(SECTIONS):
        u = x_ref[rows(s), ALL : ALL + TOKENS].astype(F32)
        w = x_ref[rows(s), ALL + TOKENS : ALL + 2 * TOKENS].astype(F32)
        if s > 0:
            before = lat[0 : RANK * s, :]
            u += dot(x_ref[rows(s), 0 : RANK * s], before)
            w += dot(xt[rows(s), 0 : RANK * s], before)
        r = lax.rsqrt(jnp.maximum(norm, 0.0) * (1.0 / WIDTH) + 1e-5)
        latent = (u * r).astype(BF16)
        lat[rows(s), :] = latent
        after = w + dot(xt[rows(s), rows(s)], latent)
        norm += jnp.sum(latent.astype(F32) * (w + after), axis=0, keepdims=True)
        wp[rows(s), :] = after
        rms[s : s + 1, :] = r

    carry = jnp.zeros((1, TOKENS), F32)
    for s in reversed(range(SECTIONS)):
        inner = x_ref[rows(s), ALL + 2 * TOKENS : XW].astype(F32) - carry * wp[rows(s), :]
        if s < SECTIONS - 1:
            later = RANK * (s + 1)
            inner += dot(xt[rows(s), later:ALL], scaled_inner[later:ALL, :])
            inner -= dot(x_ref[rows(s), later:ALL], cl[later:ALL, :])
        r = rms[s : s + 1, :]
        latent = lat[rows(s), :].astype(F32)
        scaled_inner[rows(s), :] = (r * inner).astype(BF16)
        cl[rows(s), :] = (carry * latent).astype(BF16)
        carry += r * r * (jnp.sum(latent * inner, axis=0, keepdims=True) * (1.0 / WIDTH))

    lower, upper = block_masks()
    af, bf, h = af_ref[...], bf_ref[...], h_ref[...]
    ls, ri, cls = lat[...], scaled_inner[...], cl[...]
    down = dot(ri, h) + dot(jnp.where(lower, dot(ri, ls, NT), 0.0).astype(BF16), bf) * rs
    gd_ref[...] = (down * WIDTH**-0.5).astype(BF16)
    mixed = jnp.where(upper, dot(ls, cls, NT), dot(cls, ls, NT)).astype(BF16)
    up = dot(ls, q_ref[...]) - dot(cls, h) - dot(mixed, bf) * rs
    up += dot(jnp.where(upper, dot(ls, ri, NT), 0.0).astype(BF16), af)
    gu_ref[...] = (up * rs).astype(BF16)


def chain(x, n, af, bf, h, q):
    return pl.pallas_call(
        chain_kernel,
        out_shape=(jax.ShapeDtypeStruct((ALL, SLICE), BF16),) * 2,
        in_specs=[VMEM] * 6,
        out_specs=(VMEM,) * 2,
        scratch_shapes=[
            pltpu.VMEM((ALL, ALL), BF16),
            pltpu.VMEM((ALL, TOKENS), BF16),
            pltpu.VMEM((ALL, TOKENS), BF16),
            pltpu.VMEM((ALL, TOKENS), BF16),
            pltpu.VMEM((ALL, TOKENS), F32),
            pltpu.VMEM((SECTIONS, TOKENS), F32),
        ],
        compiler_params=pltpu.CompilerParams(vmem_limit_bytes=LIMIT),
        name="chain",
    )(x, n, af, bf, h, q)


def adam(param, first, second, grad):
    first_new = 0.9 * first.astype(F32) + 0.1 * grad
    second_new = 0.999 * second.astype(F32) + 0.001 * grad * grad
    corr_one = 1.0 - 0.9**ADAM_STEP
    corr_two = 1.0 - 0.999**ADAM_STEP
    update = 0.05 * (first_new / corr_one) / (jnp.sqrt(second_new / corr_two) + 1e-08)
    return param.astype(F32) - update, first_new, second_new


def make_update(bits, number):
    near = tuple(b for b in bits if b != 4)
    steps = [(b, "split") for b in near] + [(4, "swap")] + [(b, "join") for b in reversed(near)]
    widths = {b: WIDTH >> (i + 1) for i, b in enumerate(near)}
    widths[4] = WIDTH >> len(near)

    def kernel(gd_ref, gu_ref, g_ref, a_ref, b_ref, ma_ref, mb_ref, va_ref, vb_ref, out, work, gdf, gup, sd, rd, su, ru, ss, sr, *landing):
        me, peer = lax.axis_index("section"), lax.axis_index("peer")
        land = dict(zip(near + (4,), landing))
        barrier = pltpu.get_barrier_semaphore()
        for j in range(1, SECTIONS):
            pl.semaphore_signal(barrier, inc=1, device_id=((me + j) % SECTIONS, peer), device_id_type=MESH)
        for b in bits:
            pl.semaphore_signal(barrier, inc=1, device_id=(me, peer ^ (1 << b)), device_id_type=MESH)
        pl.semaphore_wait(barrier, SECTIONS - 1 + len(bits))

        mine = pl.ds(pl.multiple_of(me * SLICE, SLICE), SLICE)
        copies = []
        for j in range(1, SECTIONS):
            to = (me + j) % SECTIONS
            rows = pl.ds(pl.multiple_of(to * RANK, RANK), RANK)
            copies.append(remote(gd_ref.at[rows], gdf.at[:, mine], sd.at[j], rd.at[j], to, peer))
            copies.append(remote(gu_ref.at[rows], gup.at[:, mine], su.at[j], ru.at[j], to, peer))
        for copy in copies:
            copy.start()
        rows = pl.ds(pl.multiple_of(me * RANK, RANK), RANK)
        gdf[:, mine] = gd_ref[rows, :]
        gup[:, mine] = gu_ref[rows, :]
        for copy in copies:
            copy.wait()

        def step(i, _):
            cols = pl.ds(pl.multiple_of(i * 512, 512), 512)
            grad = gdf[:, cols].astype(F32) * g_ref[:, cols]
            new = adam(a_ref[:, cols], ma_ref[:, cols], va_ref[:, cols], grad)
            other = adam(b_ref[:, cols], mb_ref[:, cols], vb_ref[:, cols], gup[:, cols].astype(F32))
            for k, value in enumerate((new[0], other[0], new[1], other[1], new[2], other[2])):
                work[RANK * k : RANK * k + RANK, cols] = value.astype(BF16)
            return 0

        lax.fori_loop(0, WIDTH // 512, step, 0)

        start = 0
        for number_of, (b, kind) in enumerate(steps):
            bit = (peer // (1 << b)) % 2
            to = peer + (1 - 2 * bit) * (1 << b)
            width = widths[b]
            if kind == "split":
                keep = pl.ds(pl.multiple_of(start + bit * width, width), width)
                give = pl.ds(pl.multiple_of(start + (1 - bit) * width, width), width)
                copy = remote(work.at[:, give], land[b], ss.at[number_of], sr.at[number_of], me, to)
                start = start + bit * width
            elif kind == "swap":
                keep = pl.ds(pl.multiple_of(start, width), width)
                copy = remote(work.at[:, keep], land[b], ss.at[number_of], sr.at[number_of], me, to)
            else:
                keep = pl.ds(pl.multiple_of(start, width), width)
                copy = remote(out.at[:, keep], out.at[:, keep], ss.at[number_of], sr.at[number_of], me, to)
                start = start - bit * width
            copy.start()
            copy.wait()
            if kind != "join":
                mean = ((work[:, keep].astype(F32) + land[b][...].astype(F32)) * 0.5).astype(BF16)
                if kind == "split":
                    work[:, keep] = mean
                else:
                    out[:, keep] = mean

    dma = pltpu.SemaphoreType.DMA

    def update(gd, gu, gain, *state):
        return pl.pallas_call(
            kernel,
            out_shape=jax.ShapeDtypeStruct((6 * RANK, WIDTH), BF16),
            in_specs=[VMEM] * 9,
            out_specs=VMEM,
            scratch_shapes=[pltpu.VMEM((6 * RANK, WIDTH), BF16)]
            + [pltpu.VMEM((RANK, WIDTH), BF16)] * 2
            + [dma((SECTIONS,))] * 4
            + [dma((len(steps),))] * 2
            + [pltpu.VMEM((6 * RANK, widths[b]), BF16) for b in near + (4,)],
            compiler_params=pltpu.CompilerParams(
                collective_id=1 + number, has_side_effects=True, vmem_limit_bytes=LIMIT
            ),
            name=f"update_{number}",
        )(gd, gu, gain, *state)

    return update


CASES = [(0, 4), (0, 1, 4), (0, 2, 4), (0, 3, 4), (0, 1, 2, 4), (0, 1, 3, 4), (0, 2, 3, 4)]
CASE_OF_MASK = [0, 1, 2, 4, 3, 5, 6, 0]


def on_device(hidden_in, cotangent, norm_gain, *rest):
    *state, round_bits = rest
    state = [
        jnp.swapaxes(array[0, 0], 0, 1) if number % 2 == 0 else array[0, 0] for number, array in enumerate(state)
    ]
    a, b = state[:2]
    h, q = hidden_in[0], cotangent[0]
    x, n, af, bf = products(h, q, norm_gain, a, b)
    gd, gu = chain(x, n, af, bf, h, q)
    named = [jnp.any(round_bits == bit).astype(jnp.int32) for bit in (1, 2, 3)]
    mask = named[0] + 2 * named[1] + 4 * named[2]
    case = jnp.sum(jnp.where(jnp.arange(8) == mask, jnp.array(CASE_OF_MASK), 0))
    out = lax.switch(case, [make_update(bits, i) for i, bits in enumerate(CASES)], gd, gu, norm_gain, *state)
    parts = [out[RANK * k : RANK * k + RANK] for k in range(6)]
    return tuple((jnp.swapaxes(p, 0, 1) if k % 2 == 0 else p)[None, None] for k, p in enumerate(parts))


def solution(mesh):
    held = P("section", "peer", None, None)
    return jax.shard_map(
        on_device,
        mesh=mesh,
        in_specs=(P("peer", None, "section"), P("peer", None, "section"), P("section", None)) + (held,) * 6 + (P(),),
        out_specs=(held,) * 6,
        check_vma=False,
    )
```

```python
import jax
import jax.numpy as jnp
from jax import lax
from jax.experimental import pallas as pl
from jax.experimental.pallas import tpu as pltpu
from jax.sharding import PartitionSpec as P

ADAM_STEP = 100
MESH = pl.DeviceIdType.MESH
F32, BF16 = jnp.float32, jnp.bfloat16
SECTIONS, NX, NY = 16, 4, 4
RANK, WIDTH, TOKENS = 32, 4096, 128
SLICE = WIDTH // SECTIONS
ALL = SECTIONS * RANK
XW = ALL + 3 * TOKENS
VMEM = pl.BlockSpec(memory_space=pltpu.VMEM)
LIMIT = 48 << 20

NN = (((1,), (0,)), ((), ()))
NT = (((1,), (1,)), ((), ()))


def dot(a, b, dims=NN):
    return lax.dot_general(a, b, dims, preferred_element_type=F32)


def block_masks():
    row = lax.broadcasted_iota(jnp.int32, (ALL, ALL), 0) // RANK
    col = lax.broadcasted_iota(jnp.int32, (ALL, ALL), 1) // RANK
    return row > col, row < col


def remote(src, dst, send, recv, section, peer):
    return pltpu.make_async_remote_copy(
        src_ref=src, dst_ref=dst, send_sem=send, recv_sem=recv, device_id=(section, peer), device_id_type=MESH
    )


def products_kernel(
    h_ref, q_ref, g_ref, a_ref, b_ref, x_ref, n_ref, af_ref, bf_ref,
    scaled, part, rx, px, ry, npart, nrx, npx, nry, sa, ra, sb, rb, sx, rxs, sn, rn, sy, rys, sm, rm, sg, rg, sh, rh,
):
    me, peer = lax.axis_index("section"), lax.axis_index("peer")
    mx, my = me // NY, me % NY

    barrier = pltpu.get_barrier_semaphore()
    for j in range(1, SECTIONS):
        pl.semaphore_signal(barrier, inc=1, device_id=((me + j) % SECTIONS, peer), device_id_type=MESH)
    scaled[...] = (a_ref[...].astype(F32) * (g_ref[...] * WIDTH**-0.5)).astype(BF16)
    pl.semaphore_wait(barrier, SECTIONS - 1)

    mine = pl.ds(pl.multiple_of(me * RANK, RANK), RANK)
    copies = []
    for j in range(1, SECTIONS):
        to = (me + j) % SECTIONS
        cols = pl.ds(pl.multiple_of(to * SLICE, SLICE), SLICE)
        copies.append(remote(scaled.at[:, cols], af_ref.at[mine], sa.at[j], ra.at[j], to, peer))
        copies.append(remote(b_ref.at[:, cols], bf_ref.at[mine], sb.at[j], rb.at[j], to, peer))
    for copy in copies:
        copy.start()
    cols = pl.ds(pl.multiple_of(me * SLICE, SLICE), SLICE)
    af_ref[mine, :] = scaled[:, cols]
    bf_ref[mine, :] = b_ref[:, cols]
    h = h_ref[...]
    square = h.astype(F32) * h.astype(F32)
    high = square.astype(BF16)
    low = (square - high.astype(F32)).astype(BF16)
    ones = jnp.ones((8, SLICE), BF16)
    npart[...] = dot(ones, high, NT) + dot(ones, low, NT)
    for copy in copies:
        copy.wait()

    af, bf = af_ref[...], bf_ref[...]
    rs = RANK**-0.5
    lower, _ = block_masks()
    part[:, 0:ALL] = jnp.where(lower, dot(af, bf, NT) * rs, dot(bf, bf, NT) * (1.0 / RANK)).astype(BF16)
    part[:, ALL : ALL + TOKENS] = dot(af, h, NT).astype(BF16)
    part[:, ALL + TOKENS : ALL + 2 * TOKENS] = (dot(bf, h, NT) * rs).astype(BF16)
    part[:, ALL + 2 * TOKENS : XW] = (dot(bf, q_ref[...], NT) * rs).astype(BF16)

    group = NY * RANK

    def group_rows(x):
        return pl.ds(pl.multiple_of(x * group, group), group)

    copies = []
    for j in range(1, NX):
        x = (mx + j) % NX
        copies.append(remote(part.at[group_rows(x)], rx.at[j - 1], sx.at[j], rxs.at[j], x * NY + my, peer))
        copies.append(remote(npart, nrx.at[j - 1], sn.at[j], rn.at[j], x * NY + my, peer))
    for copy in copies:
        copy.start()
    for copy in copies:
        copy.wait()
    total = part[group_rows(mx), :].astype(F32)
    for j in range(NX - 1):
        total += rx[j].astype(F32)
    px[...] = total.astype(BF16)
    npx[...] = npart[...] + nrx[0] + nrx[1] + nrx[2]

    def rank_rows(y):
        return pl.ds(pl.multiple_of(y * RANK, RANK), RANK)

    copies = []
    for j in range(1, NY):
        y = (my + j) % NY
        copies.append(remote(px.at[rank_rows(y)], ry.at[j - 1], sy.at[j], rys.at[j], mx * NY + y, peer))
        copies.append(remote(npx, nry.at[j - 1], sm.at[j], rm.at[j], mx * NY + y, peer))
    for copy in copies:
        copy.start()
    for copy in copies:
        copy.wait()
    total = px[rank_rows(my), :].astype(F32)
    for j in range(NY - 1):
        total += ry[j].astype(F32)
    x_ref[mine, :] = total.astype(BF16)
    n_ref[...] = npx[...] + nry[0] + nry[1] + nry[2]

    copies = []
    for j in range(1, NY):
        to = mx * NY + (my + j) % NY
        copies.append(remote(x_ref.at[mine], x_ref.at[mine], sg.at[j], rg.at[j], to, peer))
    for copy in copies:
        copy.start()
    for copy in copies:
        copy.wait()
    copies = []
    for j in range(1, NX):
        to = ((mx + j) % NX) * NY + my
        copies.append(remote(x_ref.at[group_rows(mx)], x_ref.at[group_rows(mx)], sh.at[j], rh.at[j], to, peer))
    for copy in copies:
        copy.start()
    for copy in copies:
        copy.wait()


def products(h, q, gain, a, b):
    dma = pltpu.SemaphoreType.DMA
    group = NY * RANK
    return pl.pallas_call(
        products_kernel,
        out_shape=(
            jax.ShapeDtypeStruct((ALL, XW), BF16),
            jax.ShapeDtypeStruct((8, TOKENS), F32),
            jax.ShapeDtypeStruct((ALL, SLICE), BF16),
            jax.ShapeDtypeStruct((ALL, SLICE), BF16),
        ),
        in_specs=[VMEM] * 5,
        out_specs=(VMEM,) * 4,
        scratch_shapes=[
            pltpu.VMEM((RANK, WIDTH), BF16),
            pltpu.VMEM((ALL, XW), BF16),
            pltpu.VMEM((NX - 1, group, XW), BF16),
            pltpu.VMEM((group, XW), BF16),
            pltpu.VMEM((NY - 1, RANK, XW), BF16),
            pltpu.VMEM((8, TOKENS), F32),
            pltpu.VMEM((NX - 1, 8, TOKENS), F32),
            pltpu.VMEM((8, TOKENS), F32),
            pltpu.VMEM((NY - 1, 8, TOKENS), F32),
        ]
        + [dma((SECTIONS,))] * 4
        + [dma((4,))] * 12,
        compiler_params=pltpu.CompilerParams(collective_id=0, has_side_effects=True, vmem_limit_bytes=LIMIT),
        name="products",
    )(h, q, gain, a, b)


def run_chain(x_ref, n_ref, af_ref, bf_ref, h_ref, q_ref, gd_ref, gu_ref, xt, lat, scaled_inner, cl, wp, rms):
    rs = RANK**-0.5
    xt[...] = x_ref[:, 0:ALL].astype(F32).T.astype(BF16)

    def rows(s):
        return slice(RANK * s, RANK * s + RANK)

    norm = n_ref[0:1, :]
    for s in range(SECTIONS):
        u = x_ref[rows(s), ALL : ALL + TOKENS].astype(F32)
        w = x_ref[rows(s), ALL + TOKENS : ALL + 2 * TOKENS].astype(F32)
        if s > 0:
            before = lat[0 : RANK * s, :]
            u += dot(x_ref[rows(s), 0 : RANK * s], before)
            w += dot(xt[rows(s), 0 : RANK * s], before)
        r = lax.rsqrt(jnp.maximum(norm, 0.0) * (1.0 / WIDTH) + 1e-5)
        latent = (u * r).astype(BF16)
        lat[rows(s), :] = latent
        after = w + dot(xt[rows(s), rows(s)], latent)
        norm += jnp.sum(latent.astype(F32) * (w + after), axis=0, keepdims=True)
        wp[rows(s), :] = after
        rms[s : s + 1, :] = r

    carry = jnp.zeros((1, TOKENS), F32)
    for s in reversed(range(SECTIONS)):
        inner = x_ref[rows(s), ALL + 2 * TOKENS : XW].astype(F32) - carry * wp[rows(s), :]
        if s < SECTIONS - 1:
            later = RANK * (s + 1)
            inner += dot(xt[rows(s), later:ALL], scaled_inner[later:ALL, :])
            inner -= dot(x_ref[rows(s), later:ALL], cl[later:ALL, :])
        r = rms[s : s + 1, :]
        latent = lat[rows(s), :].astype(F32)
        scaled_inner[rows(s), :] = (r * inner).astype(BF16)
        cl[rows(s), :] = (carry * latent).astype(BF16)
        carry += r * r * (jnp.sum(latent * inner, axis=0, keepdims=True) * (1.0 / WIDTH))

    lower, upper = block_masks()
    af, bf, h = af_ref[...], bf_ref[...], h_ref[...]
    ls, ri, cls = lat[...], scaled_inner[...], cl[...]
    down = dot(ri, h) + dot(jnp.where(lower, dot(ri, ls, NT), 0.0).astype(BF16), bf) * rs
    gd_ref[...] = (down * WIDTH**-0.5).astype(BF16)
    mixed = jnp.where(upper, dot(ls, cls, NT), dot(cls, ls, NT)).astype(BF16)
    up = dot(ls, q_ref[...]) - dot(cls, h) - dot(mixed, bf) * rs
    up += dot(jnp.where(upper, dot(ls, ri, NT), 0.0).astype(BF16), af)
    gu_ref[...] = (up * rs).astype(BF16)


CHAIN_SCRATCH = [
    pltpu.VMEM((ALL, SLICE), BF16),
    pltpu.VMEM((ALL, SLICE), BF16),
    pltpu.VMEM((ALL, ALL), BF16),
    pltpu.VMEM((ALL, TOKENS), BF16),
    pltpu.VMEM((ALL, TOKENS), BF16),
    pltpu.VMEM((ALL, TOKENS), BF16),
    pltpu.VMEM((ALL, TOKENS), F32),
    pltpu.VMEM((SECTIONS, TOKENS), F32),
]


def adam(param, first, second, grad):
    first_new = 0.9 * first.astype(F32) + 0.1 * grad
    second_new = 0.999 * second.astype(F32) + 0.001 * grad * grad
    corr_one = 1.0 - 0.9**ADAM_STEP
    corr_two = 1.0 - 0.999**ADAM_STEP
    update = 0.05 * (first_new / corr_one) / (jnp.sqrt(second_new / corr_two) + 1e-08)
    return param.astype(F32) - update, first_new, second_new


def make_update(bits, number):
    zbits = tuple(b for b in bits if b not in (0, 4))
    group = 1 << len(zbits)
    offsets = [sum(1 << b for i, b in enumerate(zbits) if m >> i & 1) for m in range(group)]
    half_width = WIDTH // 2
    first = 0 if not zbits else 1280 if zbits == (1,) else 1024
    za = first // group
    yb_width = (half_width - first) // 2
    zb = yb_width // group

    def kernel(
        x_ref, n_ref, af_ref, bf_ref, h_ref, q_ref, g_ref, *rest
    ):
        state, out, rest = rest[:6], rest[6], rest[7:]
        gd, gu, xt, lat, scaled_inner, cl, wp, rms = rest[:8]
        work, half, gdf, gup, landc, sd, rd, su, ru, sc, rc, sj, rj = rest[8:21]
        rest = rest[21:]
        me, peer = lax.axis_index("section"), lax.axis_index("peer")
        core, far = peer % 2, peer // 16
        rank = sum(((peer // (1 << b)) % 2) * (1 << i) for i, b in enumerate(zbits)) if zbits else 0

        barrier = pltpu.get_barrier_semaphore()
        for j in range(1, SECTIONS):
            pl.semaphore_signal(barrier, inc=1, device_id=((me + j) % SECTIONS, peer), device_id_type=MESH)
        partners = [1, 16] + offsets[1:]
        for offset in partners:
            pl.semaphore_signal(barrier, inc=1, device_id=(me, peer ^ offset), device_id_type=MESH)
        run_chain(x_ref, n_ref, af_ref, bf_ref, h_ref, q_ref, gd, gu, xt, lat, scaled_inner, cl, wp, rms)
        pl.semaphore_wait(barrier, SECTIONS - 1 + len(partners))

        mine = pl.ds(pl.multiple_of(me * SLICE, SLICE), SLICE)
        sends = []
        for j in range(1, SECTIONS):
            to = (me + j) % SECTIONS
            rows = pl.ds(pl.multiple_of(to * RANK, RANK), RANK)
            sends.append(remote(gd.at[rows], gdf.at[:, mine], sd.at[j], rd.at[me], to, peer))
            sends.append(remote(gu.at[rows], gup.at[:, mine], su.at[j], ru.at[me], to, peer))
        for copy in sends:
            copy.start()
        rows = pl.ds(pl.multiple_of(me * RANK, RANK), RANK)
        gdf[:, mine] = gd[rows, :]
        gup[:, mine] = gu[rows, :]

        def advance(f):
            cols = pl.ds(pl.multiple_of(f * SLICE, SLICE), SLICE)

            @pl.when(f != me)
            def _():
                remote(gd.at[0:RANK], gdf.at[:, cols], sd.at[0], rd.at[f], me, peer).wait_recv()
                remote(gu.at[0:RANK], gup.at[:, cols], su.at[0], ru.at[f], me, peer).wait_recv()

            a_ref, b_ref, ma_ref, mb_ref, va_ref, vb_ref = state
            grad = gdf[:, cols].astype(F32) * g_ref[:, cols]
            new = adam(a_ref[:, cols], ma_ref[:, cols], va_ref[:, cols], grad)
            other = adam(b_ref[:, cols], mb_ref[:, cols], vb_ref[:, cols], gup[:, cols].astype(F32))
            for k, value in enumerate((new[0], other[0], new[1], other[1], new[2], other[2])):
                work[RANK * k : RANK * k + RANK, cols] = value.astype(BF16)
            return cols

        def core_copy(k):
            cols = pl.ds(pl.multiple_of(((1 - core) * 8 + k) * SLICE, SLICE), SLICE)
            there = pl.ds(pl.multiple_of(k * SLICE, SLICE), SLICE)
            return remote(work.at[:, cols], landc.at[:, there], sc.at[k], rc.at[k], me, peer ^ 1)

        def give(i, _):
            k = (me + i) % 8
            advance((1 - core) * 8 + k)
            core_copy(k).start()
            return 0

        def keep(i, _):
            k = (me + i) % 8
            cols = advance(core * 8 + k)
            copy = core_copy(k)
            copy.wait_recv()
            here = pl.ds(pl.multiple_of(k * SLICE, SLICE), SLICE)
            half[:, here] = ((work[:, cols].astype(F32) + landc[:, here].astype(F32)) * 0.5).astype(BF16)
            return 0

        lax.fori_loop(0, 8, give, 0)
        lax.fori_loop(0, 8, keep, 0)

        def mean(*values):
            total = values[0].astype(F32)
            for value in values[1:]:
                total += value.astype(F32)
            return (total * (1.0 / len(values))).astype(BF16)

        def cols_at(at, width):
            return pl.ds(pl.multiple_of(at, 128), width)

        base = core * half_width
        pending = []
        joins = iter(range(4))

        def join(cols):
            k = next(joins)
            copy = remote(out.at[:, cols], out.at[:, cols], sj.at[k], rj.at[k], me, peer ^ 1)
            copy.start()
            pending.append(copy)

        if not zbits:
            land_y, sy, ry = rest
            parts = 4
            width = half_width // parts
            swaps = []
            for k in range(parts):
                cols = pl.ds(k * width, width)
                copy = remote(half.at[:, cols], land_y.at[:, cols], sy.at[k], ry.at[k], me, peer ^ 16)
                copy.start()
                swaps.append(copy)
            for k in range(parts):
                cols = pl.ds(k * width, width)
                swaps[k].wait()
                there = cols_at(base + k * width, width)
                out[:, there] = mean(half[:, cols], land_y[:, cols])
                join(there)
        else:
            land_a, land_a2, acc_a, land_b, land_b2, acc_b, sems_s, sems_r = rest
            count = iter(range(32))

            def send(src, dst, offset):
                k = next(count)
                copy = remote(src, dst, sems_s.at[k], sems_r.at[k], me, peer ^ offset)
                copy.start()
                return copy

            y_split = send(half.at[:, cols_at(first + (1 - far) * yb_width, yb_width)], land_b, 16)
            z_split = [
                send(half.at[:, cols_at((rank ^ m) * za, za)], land_a.at[m - 1], offsets[m]) for m in range(1, group)
            ]
            for copy in z_split:
                copy.wait()
            acc_a[...] = mean(half[:, cols_at(rank * za, za)], *[land_a[m] for m in range(group - 1)])
            y_swap = send(acc_a, land_a2, 16)
            y_split.wait()
            acc_b[...] = mean(half[:, cols_at(first + far * yb_width, yb_width)], land_b[...])
            z_swap = [
                send(acc_b.at[:, cols_at((rank ^ m) * zb, zb)] if group > 2 else acc_b, land_b2.at[m - 1], offsets[m])
                for m in range(1, group)
            ]
            b_here = cols_at(base + first + far * yb_width, yb_width)
            b_part = cols_at(base + first + far * yb_width + rank * zb, zb) if group > 2 else b_here
            a_part = cols_at(base + rank * za, za)
            for copy in z_swap:
                copy.wait()
            own = acc_b[:, cols_at(rank * zb, zb)] if group > 2 else acc_b[...]
            out[:, b_part] = mean(own, *[land_b2[m] for m in range(group - 1)])
            if group > 2:
                z_back = [send(out.at[:, b_part], out.at[:, b_part], offsets[m]) for m in range(1, group)]
                for copy in z_back:
                    copy.wait()
            y_join = send(out.at[:, b_here], out.at[:, b_here], 16)
            y_swap.wait()
            out[:, a_part] = mean(acc_a[...], land_a2[...])
            z_join = [send(out.at[:, a_part], out.at[:, a_part], offsets[m]) for m in range(1, group)]
            y_join.wait()
            join(cols_at(base + first, half_width - first))
            for copy in z_join:
                copy.wait()
            join(cols_at(base, first))
        for copy in pending:
            copy.wait()
        for copy in sends:
            copy.wait_send()

        def sent(k, _):
            core_copy(k).wait_send()
            return 0

        lax.fori_loop(0, 8, sent, 0)

    dma = pltpu.SemaphoreType.DMA
    rows = 6 * RANK
    scratch = CHAIN_SCRATCH + [
        pltpu.VMEM((rows, WIDTH), BF16),
        pltpu.VMEM((rows, half_width), BF16),
        pltpu.VMEM((RANK, WIDTH), BF16),
        pltpu.VMEM((RANK, WIDTH), BF16),
        pltpu.VMEM((rows, half_width), BF16),
    ]
    scratch += [dma((SECTIONS,))] * 4 + [dma((8,))] * 2 + [dma((4,))] * 2
    if not zbits:
        scratch += [pltpu.VMEM((rows, half_width), BF16), dma((4,)), dma((4,))]
    else:
        scratch += [
            pltpu.VMEM((group - 1, rows, za), BF16),
            pltpu.VMEM((rows, za), BF16),
            pltpu.VMEM((rows, za), BF16),
            pltpu.VMEM((rows, yb_width), BF16),
            pltpu.VMEM((group - 1, rows, zb if group > 2 else yb_width), BF16),
            pltpu.VMEM((rows, yb_width), BF16),
            dma((16,)),
            dma((16,)),
        ]

    def update(*operands):
        return pl.pallas_call(
            kernel,
            out_shape=jax.ShapeDtypeStruct((rows, WIDTH), BF16),
            in_specs=[VMEM] * 13,
            out_specs=VMEM,
            scratch_shapes=scratch,
            compiler_params=pltpu.CompilerParams(
                collective_id=1 + number, has_side_effects=True, vmem_limit_bytes=LIMIT
            ),
            name=f"update_{number}",
        )(*operands)

    return update


CASES = [(0, 4), (0, 1, 4), (0, 2, 4), (0, 1, 2, 4), (0, 3, 4), (0, 1, 3, 4), (0, 2, 3, 4)]


def on_device(hidden_in, cotangent, norm_gain, *rest):
    *state, round_bits = rest
    state = [
        jnp.swapaxes(array[0, 0], 0, 1) if number % 2 == 0 else array[0, 0] for number, array in enumerate(state)
    ]
    a, b = state[:2]
    h, q = hidden_in[0], cotangent[0]
    x, n, af, bf = products(h, q, norm_gain, a, b)
    mask = lax.reduce(jnp.left_shift(jnp.int32(1), round_bits), jnp.int32(0), lax.bitwise_or, (0,))
    case = jnp.bitwise_and(jnp.right_shift(mask, 1), 7)
    branches = [make_update(bits, i) for i, bits in enumerate(CASES)]
    out = lax.switch(case, branches, x, n, af, bf, h, q, norm_gain, *state)
    parts = [out[RANK * k : RANK * k + RANK] for k in range(6)]
    return tuple((jnp.swapaxes(p, 0, 1) if k % 2 == 0 else p)[None, None] for k, p in enumerate(parts))


def solution(mesh):
    held = P("section", "peer", None, None)
    return jax.shard_map(
        on_device,
        mesh=mesh,
        in_specs=(P("peer", None, "section"), P("peer", None, "section"), P("section", None)) + (held,) * 6 + (P(),),
        out_specs=(held,) * 6,
        check_vma=False,
    )
```

```python
import jax
import jax.numpy as jnp
from jax import lax
from jax.experimental import pallas as pl
from jax.experimental.pallas import tpu as pltpu
from jax.sharding import PartitionSpec as P

ADAM_STEP = 100
MESH = pl.DeviceIdType.MESH
F32, BF16 = jnp.float32, jnp.bfloat16
SECTIONS, NX, NY = 16, 4, 4
RANK, WIDTH, TOKENS = 32, 4096, 128
SLICE = WIDTH // SECTIONS
ALL = SECTIONS * RANK
XW = ALL + 3 * TOKENS
VMEM = pl.BlockSpec(memory_space=pltpu.VMEM)
LIMIT = 48 << 20

NN = (((1,), (0,)), ((), ()))
NT = (((1,), (1,)), ((), ()))


def dot(a, b, dims=NN):
    return lax.dot_general(a, b, dims, preferred_element_type=F32)


def block_masks():
    row = lax.broadcasted_iota(jnp.int32, (ALL, ALL), 0) // RANK
    col = lax.broadcasted_iota(jnp.int32, (ALL, ALL), 1) // RANK
    return row > col, row < col


def remote(src, dst, send, recv, section, peer):
    return pltpu.make_async_remote_copy(
        src_ref=src, dst_ref=dst, send_sem=send, recv_sem=recv, device_id=(section, peer), device_id_type=MESH
    )


CHUNKS = ((ALL + TOKENS, 2 * TOKENS), (ALL // 2, ALL // 2 + TOKENS), (0, ALL // 2))


def products_kernel(
    h_ref, q_ref, g_ref, a_ref, b_ref, x_ref, n_ref, af_ref, bf_ref,
    scaled, part, rx, px, ry, npart, nrx, npx, nry, sa, ra, sb, rb, sx, rxs, sy, rys, sg, rg, sh, rh, sn, rn, sm, rm,
):
    me, peer = lax.axis_index("section"), lax.axis_index("peer")
    mx, my = me // NY, me % NY

    barrier = pltpu.get_barrier_semaphore()
    for j in range(1, SECTIONS):
        pl.semaphore_signal(barrier, inc=1, device_id=((me + j) % SECTIONS, peer), device_id_type=MESH)
    scaled[...] = (a_ref[...].astype(F32) * (g_ref[...] * WIDTH**-0.5)).astype(BF16)
    pl.semaphore_wait(barrier, SECTIONS - 1)

    mine = pl.ds(pl.multiple_of(me * RANK, RANK), RANK)

    def scatter(src, dst, send, recv):
        copies = []
        for j in range(1, SECTIONS):
            to = (me + j) % SECTIONS
            cols = pl.ds(pl.multiple_of(to * SLICE, SLICE), SLICE)
            copies.append(remote(src.at[:, cols], dst.at[mine], send.at[j], recv.at[j], to, peer))
        for copy in copies:
            copy.start()
        return copies

    b_copies = scatter(b_ref, bf_ref, sb, rb)
    a_copies = scatter(scaled, af_ref, sa, ra)
    cols = pl.ds(pl.multiple_of(me * SLICE, SLICE), SLICE)
    af_ref[mine, :] = scaled[:, cols]
    bf_ref[mine, :] = b_ref[:, cols]
    h = h_ref[...]
    square = h.astype(F32) * h.astype(F32)
    high = square.astype(BF16)
    low = (square - high.astype(F32)).astype(BF16)
    ones = jnp.ones((8, SLICE), BF16)
    npart[...] = dot(ones, high, NT) + dot(ones, low, NT)
    rs = RANK**-0.5

    def group_rows(x):
        return pl.ds(pl.multiple_of(x * NY * RANK, NY * RANK), NY * RANK)

    def rank_rows(y):
        return pl.ds(pl.multiple_of(y * RANK, RANK), RANK)

    held = [pl.ds(at, width) for at, width in CHUNKS]
    flying = [None] * len(CHUNKS)

    def started(copies):
        for copy in copies:
            copy.start()
        return copies

    def landed(c):
        for copy in flying[c]:
            copy.wait()

    def reduce_x(c):
        copies = []
        for j in range(1, NX):
            x, k = (mx + j) % NX, 4 * c + j
            to = x * NY + my
            copies.append(remote(part.at[group_rows(x), held[c]], rx.at[j - 1, :, held[c]], sx.at[k], rxs.at[k], to, peer))
            if c == 0:
                copies.append(remote(npart, nrx.at[j - 1], sn.at[j], rn.at[j], to, peer))
        flying[c] = started(copies)

    def reduce_y(c):
        landed(c)
        total = part[group_rows(mx), held[c]].astype(F32)
        for j in range(NX - 1):
            total += rx[j, :, held[c]].astype(F32)
        px[:, held[c]] = total.astype(BF16)
        if c == 0:
            npx[...] = npart[...] + nrx[0] + nrx[1] + nrx[2]
        copies = []
        for j in range(1, NY):
            y, k = (my + j) % NY, 4 * c + j
            to = mx * NY + y
            copies.append(remote(px.at[rank_rows(y), held[c]], ry.at[j - 1, :, held[c]], sy.at[k], rys.at[k], to, peer))
            if c == 0:
                copies.append(remote(npx, nry.at[j - 1], sm.at[j], rm.at[j], to, peer))
        flying[c] = started(copies)

    def gather_y(c):
        landed(c)
        total = px[rank_rows(my), held[c]].astype(F32)
        for j in range(NY - 1):
            total += ry[j, :, held[c]].astype(F32)
        x_ref[mine, held[c]] = total.astype(BF16)
        if c == 0:
            n_ref[...] = npx[...] + nry[0] + nry[1] + nry[2]
        rows = x_ref.at[mine, held[c]]
        flying[c] = started(
            [
                remote(rows, rows, sg.at[4 * c + j], rg.at[4 * c + j], mx * NY + (my + j) % NY, peer)
                for j in range(1, NY)
            ]
        )

    def gather_x(c):
        landed(c)
        rows = x_ref.at[group_rows(mx), held[c]]
        flying[c] = started(
            [
                remote(rows, rows, sh.at[4 * c + j], rh.at[4 * c + j], ((mx + j) % NX) * NY + my, peer)
                for j in range(1, NX)
            ]
        )

    for copy in b_copies:
        copy.wait()
    bf = bf_ref[...]
    part[:, ALL + TOKENS : ALL + 2 * TOKENS] = (dot(bf, h, NT) * rs).astype(BF16)
    part[:, ALL + 2 * TOKENS : XW] = (dot(bf, q_ref[...], NT) * rs).astype(BF16)
    reduce_x(0)
    for copy in a_copies:
        copy.wait()
    af = af_ref[...]
    lower, _ = block_masks()

    def squares(at):
        other = bf_ref[at : at + ALL // 2, :]
        mask = lower[:, at : at + ALL // 2]
        products = jnp.where(mask, dot(af, other, NT) * rs, dot(bf, other, NT) * (1.0 / RANK))
        part[:, at : at + ALL // 2] = products.astype(BF16)

    part[:, ALL : ALL + TOKENS] = dot(af, h, NT).astype(BF16)
    squares(ALL // 2)
    reduce_x(1)
    squares(0)
    reduce_x(2)
    reduce_y(0)
    reduce_y(1)
    gather_y(0)
    reduce_y(2)
    gather_y(1)
    gather_x(0)
    gather_y(2)
    gather_x(1)
    gather_x(2)
    for c in range(len(CHUNKS)):
        landed(c)


def products(h, q, gain, a, b):
    dma = pltpu.SemaphoreType.DMA
    group = NY * RANK
    return pl.pallas_call(
        products_kernel,
        out_shape=(
            jax.ShapeDtypeStruct((ALL, XW), BF16),
            jax.ShapeDtypeStruct((8, TOKENS), F32),
            jax.ShapeDtypeStruct((ALL, SLICE), BF16),
            jax.ShapeDtypeStruct((ALL, SLICE), BF16),
        ),
        in_specs=[VMEM] * 5,
        out_specs=(VMEM,) * 4,
        scratch_shapes=[
            pltpu.VMEM((RANK, WIDTH), BF16),
            pltpu.VMEM((ALL, XW), BF16),
            pltpu.VMEM((NX - 1, group, XW), BF16),
            pltpu.VMEM((group, XW), BF16),
            pltpu.VMEM((NY - 1, RANK, XW), BF16),
            pltpu.VMEM((8, TOKENS), F32),
            pltpu.VMEM((NX - 1, 8, TOKENS), F32),
            pltpu.VMEM((8, TOKENS), F32),
            pltpu.VMEM((NY - 1, 8, TOKENS), F32),
        ]
        + [dma((SECTIONS,))] * 4
        + [dma((4 * len(CHUNKS),))] * 8
        + [dma((4,))] * 4,
        compiler_params=pltpu.CompilerParams(collective_id=0, has_side_effects=True, vmem_limit_bytes=LIMIT),
        name="products",
    )(h, q, gain, a, b)


def run_chain(x_ref, n_ref, af_ref, bf_ref, h_ref, q_ref, gd_ref, gu_ref, xt, lat, scaled_inner, cl, wp, rms):
    rs = RANK**-0.5
    xt[...] = x_ref[:, 0:ALL].astype(F32).T.astype(BF16)

    def rows(s):
        return slice(RANK * s, RANK * s + RANK)

    norm = n_ref[0:1, :]
    for s in range(SECTIONS):
        u = x_ref[rows(s), ALL : ALL + TOKENS].astype(F32)
        w = x_ref[rows(s), ALL + TOKENS : ALL + 2 * TOKENS].astype(F32)
        if s > 0:
            before = lat[0 : RANK * s, :]
            u += dot(x_ref[rows(s), 0 : RANK * s], before)
            w += dot(xt[rows(s), 0 : RANK * s], before)
        r = lax.rsqrt(jnp.maximum(norm, 0.0) * (1.0 / WIDTH) + 1e-5)
        latent = (u * r).astype(BF16)
        lat[rows(s), :] = latent
        after = w + dot(xt[rows(s), rows(s)], latent)
        norm += jnp.sum(latent.astype(F32) * (w + after), axis=0, keepdims=True)
        wp[rows(s), :] = after
        rms[s : s + 1, :] = r

    carry = jnp.zeros((1, TOKENS), F32)
    for s in reversed(range(SECTIONS)):
        inner = x_ref[rows(s), ALL + 2 * TOKENS : XW].astype(F32) - carry * wp[rows(s), :]
        if s < SECTIONS - 1:
            later = RANK * (s + 1)
            inner += dot(xt[rows(s), later:ALL], scaled_inner[later:ALL, :])
            inner -= dot(x_ref[rows(s), later:ALL], cl[later:ALL, :])
        r = rms[s : s + 1, :]
        latent = lat[rows(s), :].astype(F32)
        scaled_inner[rows(s), :] = (r * inner).astype(BF16)
        cl[rows(s), :] = (carry * latent).astype(BF16)
        carry += r * r * (jnp.sum(latent * inner, axis=0, keepdims=True) * (1.0 / WIDTH))

    lower, upper = block_masks()
    af, bf, h = af_ref[...], bf_ref[...], h_ref[...]
    ls, ri, cls = lat[...], scaled_inner[...], cl[...]
    down = dot(ri, h) + dot(jnp.where(lower, dot(ri, ls, NT), 0.0).astype(BF16), bf) * rs
    gd_ref[...] = (down * WIDTH**-0.5).astype(BF16)
    mixed = jnp.where(upper, dot(ls, cls, NT), dot(cls, ls, NT)).astype(BF16)
    up = dot(ls, q_ref[...]) - dot(cls, h) - dot(mixed, bf) * rs
    up += dot(jnp.where(upper, dot(ls, ri, NT), 0.0).astype(BF16), af)
    gu_ref[...] = (up * rs).astype(BF16)


CHAIN_SCRATCH = [
    pltpu.VMEM((ALL, SLICE), BF16),
    pltpu.VMEM((ALL, SLICE), BF16),
    pltpu.VMEM((ALL, ALL), BF16),
    pltpu.VMEM((ALL, TOKENS), BF16),
    pltpu.VMEM((ALL, TOKENS), BF16),
    pltpu.VMEM((ALL, TOKENS), BF16),
    pltpu.VMEM((ALL, TOKENS), F32),
    pltpu.VMEM((SECTIONS, TOKENS), F32),
]


def adam(param, first, second, grad):
    first_new = 0.9 * first.astype(F32) + 0.1 * grad
    second_new = 0.999 * second.astype(F32) + 0.001 * grad * grad
    corr_one = 1.0 - 0.9**ADAM_STEP
    corr_two = 1.0 - 0.999**ADAM_STEP
    update = 0.05 * (first_new / corr_one) / (jnp.sqrt(second_new / corr_two) + 1e-08)
    return param.astype(F32) - update, first_new, second_new


def make_update(bits, number):
    zbits = tuple(b for b in bits if b not in (0, 4))
    group = 1 << len(zbits)
    offsets = [sum(1 << b for i, b in enumerate(zbits) if m >> i & 1) for m in range(group)]
    half_width = WIDTH // 2
    first = 0 if not zbits else 1280 if zbits == (1,) else 1024
    za = first // group
    yb_width = (half_width - first) // 2
    zb = yb_width // group

    def kernel(
        x_ref, n_ref, af_ref, bf_ref, h_ref, q_ref, g_ref, *rest
    ):
        state, out, rest = rest[:6], rest[6], rest[7:]
        gd, gu, xt, lat, scaled_inner, cl, wp, rms = rest[:8]
        work, half, gdf, gup, landc, sd, rd, su, ru, sc, rc, sj, rj = rest[8:21]
        rest = rest[21:]
        me, peer = lax.axis_index("section"), lax.axis_index("peer")
        core, far = peer % 2, peer // 16
        rank = sum(((peer // (1 << b)) % 2) * (1 << i) for i, b in enumerate(zbits)) if zbits else 0

        barrier = pltpu.get_barrier_semaphore()
        for j in range(1, SECTIONS):
            pl.semaphore_signal(barrier, inc=1, device_id=((me + j) % SECTIONS, peer), device_id_type=MESH)
        partners = [1, 16] + offsets[1:]
        for offset in partners:
            pl.semaphore_signal(barrier, inc=1, device_id=(me, peer ^ offset), device_id_type=MESH)
        run_chain(x_ref, n_ref, af_ref, bf_ref, h_ref, q_ref, gd, gu, xt, lat, scaled_inner, cl, wp, rms)
        pl.semaphore_wait(barrier, SECTIONS - 1 + len(partners))

        mine = pl.ds(pl.multiple_of(me * SLICE, SLICE), SLICE)
        sends = []
        for j in range(1, SECTIONS):
            to = (me + j) % SECTIONS
            rows = pl.ds(pl.multiple_of(to * RANK, RANK), RANK)
            sends.append(remote(gd.at[rows], gdf.at[:, mine], sd.at[j], rd.at[me], to, peer))
            sends.append(remote(gu.at[rows], gup.at[:, mine], su.at[j], ru.at[me], to, peer))
        for copy in sends:
            copy.start()
        rows = pl.ds(pl.multiple_of(me * RANK, RANK), RANK)
        gdf[:, mine] = gd[rows, :]
        gup[:, mine] = gu[rows, :]

        def advance(f):
            cols = pl.ds(pl.multiple_of(f * SLICE, SLICE), SLICE)

            @pl.when(f != me)
            def _():
                remote(gd.at[0:RANK], gdf.at[:, cols], sd.at[0], rd.at[f], me, peer).wait_recv()
                remote(gu.at[0:RANK], gup.at[:, cols], su.at[0], ru.at[f], me, peer).wait_recv()

            a_ref, b_ref, ma_ref, mb_ref, va_ref, vb_ref = state
            grad = gdf[:, cols].astype(F32) * g_ref[:, cols]
            new = adam(a_ref[:, cols], ma_ref[:, cols], va_ref[:, cols], grad)
            other = adam(b_ref[:, cols], mb_ref[:, cols], vb_ref[:, cols], gup[:, cols].astype(F32))
            for k, value in enumerate((new[0], other[0], new[1], other[1], new[2], other[2])):
                work[RANK * k : RANK * k + RANK, cols] = value.astype(BF16)
            return cols

        def core_copy(k):
            cols = pl.ds(pl.multiple_of(((1 - core) * 8 + k) * SLICE, SLICE), SLICE)
            there = pl.ds(pl.multiple_of(k * SLICE, SLICE), SLICE)
            return remote(work.at[:, cols], landc.at[:, there], sc.at[k], rc.at[k], me, peer ^ 1)

        def give(i, _):
            k = (me + i) % 8
            advance((1 - core) * 8 + k)
            core_copy(k).start()
            return 0

        def keep(i, _):
            k = (me + i) % 8
            cols = advance(core * 8 + k)
            copy = core_copy(k)
            copy.wait_recv()
            here = pl.ds(pl.multiple_of(k * SLICE, SLICE), SLICE)
            half[:, here] = ((work[:, cols].astype(F32) + landc[:, here].astype(F32)) * 0.5).astype(BF16)
            return 0

        lax.fori_loop(0, 8, give, 0)
        lax.fori_loop(0, 8, keep, 0)

        def mean(*values):
            total = values[0].astype(F32)
            for value in values[1:]:
                total += value.astype(F32)
            return (total * (1.0 / len(values))).astype(BF16)

        def cols_at(at, width):
            return pl.ds(pl.multiple_of(at, 128), width)

        base = core * half_width
        pending = []
        joins = iter(range(4))

        def join(cols):
            k = next(joins)
            copy = remote(out.at[:, cols], out.at[:, cols], sj.at[k], rj.at[k], me, peer ^ 1)
            copy.start()
            pending.append(copy)

        if not zbits:
            land_y, sy, ry = rest
            parts = 4
            width = half_width // parts
            swaps = []
            for k in range(parts):
                cols = pl.ds(k * width, width)
                copy = remote(half.at[:, cols], land_y.at[:, cols], sy.at[k], ry.at[k], me, peer ^ 16)
                copy.start()
                swaps.append(copy)
            for k in range(parts):
                cols = pl.ds(k * width, width)
                swaps[k].wait()
                there = cols_at(base + k * width, width)
                out[:, there] = mean(half[:, cols], land_y[:, cols])
                join(there)
        else:
            land_a, land_a2, acc_a, land_b, land_b2, acc_b, sems_s, sems_r = rest
            count = iter(range(32))

            def send(src, dst, offset):
                k = next(count)
                copy = remote(src, dst, sems_s.at[k], sems_r.at[k], me, peer ^ offset)
                copy.start()
                return copy

            y_split = send(half.at[:, cols_at(first + (1 - far) * yb_width, yb_width)], land_b, 16)
            z_split = [
                send(half.at[:, cols_at((rank ^ m) * za, za)], land_a.at[m - 1], offsets[m]) for m in range(1, group)
            ]
            for copy in z_split:
                copy.wait()
            acc_a[...] = mean(half[:, cols_at(rank * za, za)], *[land_a[m] for m in range(group - 1)])
            y_swap = send(acc_a, land_a2, 16)
            y_split.wait()
            acc_b[...] = mean(half[:, cols_at(first + far * yb_width, yb_width)], land_b[...])
            z_swap = [
                send(acc_b.at[:, cols_at((rank ^ m) * zb, zb)] if group > 2 else acc_b, land_b2.at[m - 1], offsets[m])
                for m in range(1, group)
            ]
            b_here = cols_at(base + first + far * yb_width, yb_width)
            b_part = cols_at(base + first + far * yb_width + rank * zb, zb) if group > 2 else b_here
            a_part = cols_at(base + rank * za, za)
            for copy in z_swap:
                copy.wait()
            own = acc_b[:, cols_at(rank * zb, zb)] if group > 2 else acc_b[...]
            out[:, b_part] = mean(own, *[land_b2[m] for m in range(group - 1)])
            if group > 2:
                z_back = [send(out.at[:, b_part], out.at[:, b_part], offsets[m]) for m in range(1, group)]
                for copy in z_back:
                    copy.wait()
            y_join = send(out.at[:, b_here], out.at[:, b_here], 16)
            y_swap.wait()
            out[:, a_part] = mean(acc_a[...], land_a2[...])
            z_join = [send(out.at[:, a_part], out.at[:, a_part], offsets[m]) for m in range(1, group)]
            y_join.wait()
            join(cols_at(base + first, half_width - first))
            for copy in z_join:
                copy.wait()
            join(cols_at(base, first))
        for copy in pending:
            copy.wait()
        for copy in sends:
            copy.wait_send()

        def sent(k, _):
            core_copy(k).wait_send()
            return 0

        lax.fori_loop(0, 8, sent, 0)

    dma = pltpu.SemaphoreType.DMA
    rows = 6 * RANK
    scratch = CHAIN_SCRATCH + [
        pltpu.VMEM((rows, WIDTH), BF16),
        pltpu.VMEM((rows, half_width), BF16),
        pltpu.VMEM((RANK, WIDTH), BF16),
        pltpu.VMEM((RANK, WIDTH), BF16),
        pltpu.VMEM((rows, half_width), BF16),
    ]
    scratch += [dma((SECTIONS,))] * 4 + [dma((8,))] * 2 + [dma((4,))] * 2
    if not zbits:
        scratch += [pltpu.VMEM((rows, half_width), BF16), dma((4,)), dma((4,))]
    else:
        scratch += [
            pltpu.VMEM((group - 1, rows, za), BF16),
            pltpu.VMEM((rows, za), BF16),
            pltpu.VMEM((rows, za), BF16),
            pltpu.VMEM((rows, yb_width), BF16),
            pltpu.VMEM((group - 1, rows, zb if group > 2 else yb_width), BF16),
            pltpu.VMEM((rows, yb_width), BF16),
            dma((16,)),
            dma((16,)),
        ]

    def update(*operands):
        return pl.pallas_call(
            kernel,
            out_shape=jax.ShapeDtypeStruct((rows, WIDTH), BF16),
            in_specs=[VMEM] * 13,
            out_specs=VMEM,
            scratch_shapes=scratch,
            compiler_params=pltpu.CompilerParams(
                collective_id=1 + number, has_side_effects=True, vmem_limit_bytes=LIMIT
            ),
            name=f"update_{number}",
        )(*operands)

    return update


CASES = [(0, 4), (0, 1, 4), (0, 2, 4), (0, 1, 2, 4), (0, 3, 4), (0, 1, 3, 4), (0, 2, 3, 4)]


def on_device(hidden_in, cotangent, norm_gain, *rest):
    *state, round_bits = rest
    state = [
        jnp.swapaxes(array[0, 0], 0, 1) if number % 2 == 0 else array[0, 0] for number, array in enumerate(state)
    ]
    a, b = state[:2]
    h, q = hidden_in[0], cotangent[0]
    x, n, af, bf = products(h, q, norm_gain, a, b)
    mask = lax.reduce(jnp.left_shift(jnp.int32(1), round_bits), jnp.int32(0), lax.bitwise_or, (0,))
    case = jnp.bitwise_and(jnp.right_shift(mask, 1), 7)
    branches = [make_update(bits, i) for i, bits in enumerate(CASES)]
    out = lax.switch(case, branches, x, n, af, bf, h, q, norm_gain, *state)
    parts = [out[RANK * k : RANK * k + RANK] for k in range(6)]
    return tuple((jnp.swapaxes(p, 0, 1) if k % 2 == 0 else p)[None, None] for k, p in enumerate(parts))


def solution(mesh):
    held = P("section", "peer", None, None)
    return jax.shard_map(
        on_device,
        mesh=mesh,
        in_specs=(P("peer", None, "section"), P("peer", None, "section"), P("section", None)) + (held,) * 6 + (P(),),
        out_specs=(held,) * 6,
        check_vma=False,
    )
```

```python
import jax
import jax.numpy as jnp
from jax import lax
from jax.experimental import pallas as pl
from jax.experimental.pallas import tpu as pltpu
from jax.sharding import PartitionSpec as P

ADAM_STEP = 100
MESH = pl.DeviceIdType.MESH
F32, BF16 = jnp.float32, jnp.bfloat16
SECTIONS, NX, NY = 16, 4, 4
RANK, WIDTH, TOKENS = 32, 4096, 128
SLICE = WIDTH // SECTIONS
ALL = SECTIONS * RANK
XW = ALL + 3 * TOKENS
VMEM = pl.BlockSpec(memory_space=pltpu.VMEM)
SMEM = pl.BlockSpec(memory_space=pltpu.SMEM)
LIMIT = 48 << 20

NN = (((1,), (0,)), ((), ()))
NT = (((1,), (1,)), ((), ()))


def dot(a, b, dims=NN):
    return lax.dot_general(a, b, dims, preferred_element_type=F32)


def block_masks():
    row = lax.broadcasted_iota(jnp.int32, (ALL, ALL), 0) // RANK
    col = lax.broadcasted_iota(jnp.int32, (ALL, ALL), 1) // RANK
    return row > col, row < col


def remote(src, dst, send, recv, section, peer):
    return pltpu.make_async_remote_copy(
        src_ref=src, dst_ref=dst, send_sem=send, recv_sem=recv, device_id=(section, peer), device_id_type=MESH
    )


CHUNKS = ((ALL + TOKENS, 2 * TOKENS), (ALL // 2, ALL // 2 + TOKENS), (0, ALL // 2))


def products_kernel(
    bits_ref, h_hbm, q_hbm, g_hbm, a_hbm, b_hbm, case_ref, x_ref, n_ref, af_ref, bf_ref,
    h_ref, q_ref, g_ref, a_ref, b_ref, loaded, scaled, part, rx, px, ry, npart, nrx, npx, nry, sa, ra, sb, rb, sx, rxs, sy, rys, sg, rg, sh, rh, sn, rn, sm, rm,
):
    me, peer = lax.axis_index("section"), lax.axis_index("peer")
    mx, my = me // NY, me % NY

    operands = [(a_hbm, a_ref), (g_hbm, g_ref), (b_hbm, b_ref), (h_hbm, h_ref), (q_hbm, q_ref)]
    loads = [pltpu.make_async_copy(src, dst, loaded.at[k]) for k, (src, dst) in enumerate(operands)]
    for load in loads:
        load.start()
    barrier = pltpu.get_barrier_semaphore()
    for j in range(1, SECTIONS):
        pl.semaphore_signal(barrier, inc=1, device_id=((me + j) % SECTIONS, peer), device_id_type=MESH)
    case_ref[0] = sum(
        jnp.maximum(
            jnp.maximum((bits_ref[0] == bit).astype(jnp.int32), (bits_ref[1] == bit).astype(jnp.int32)),
            jnp.maximum((bits_ref[2] == bit).astype(jnp.int32), (bits_ref[3] == bit).astype(jnp.int32)),
        )
        << (bit - 1)
        for bit in (1, 2, 3)
    )
    for load in loads:
        load.wait()
    scaled[...] = (a_ref[...].astype(F32) * (g_ref[...] * WIDTH**-0.5)).astype(BF16)
    pl.semaphore_wait(barrier, SECTIONS - 1)

    mine = pl.ds(pl.multiple_of(me * RANK, RANK), RANK)

    def scatter(src, dst, send, recv):
        copies = []
        for j in range(1, SECTIONS):
            to = (me + j) % SECTIONS
            cols = pl.ds(pl.multiple_of(to * SLICE, SLICE), SLICE)
            copies.append(remote(src.at[:, cols], dst.at[mine], send.at[j], recv.at[j], to, peer))
        for copy in copies:
            copy.start()
        return copies

    b_copies = scatter(b_ref, bf_ref, sb, rb)
    a_copies = scatter(scaled, af_ref, sa, ra)
    cols = pl.ds(pl.multiple_of(me * SLICE, SLICE), SLICE)
    af_ref[mine, :] = scaled[:, cols]
    bf_ref[mine, :] = b_ref[:, cols]
    h = h_ref[...]
    square = h.astype(F32) * h.astype(F32)
    high = square.astype(BF16)
    low = (square - high.astype(F32)).astype(BF16)
    ones = jnp.ones((8, SLICE), BF16)
    npart[...] = dot(ones, high, NT) + dot(ones, low, NT)
    rs = RANK**-0.5

    def group_rows(x):
        return pl.ds(pl.multiple_of(x * NY * RANK, NY * RANK), NY * RANK)

    def rank_rows(y):
        return pl.ds(pl.multiple_of(y * RANK, RANK), RANK)

    held = [pl.ds(at, width) for at, width in CHUNKS]
    flying = [None] * len(CHUNKS)

    def started(copies):
        for copy in copies:
            copy.start()
        return copies

    def landed(c):
        for copy in flying[c]:
            copy.wait()

    def reduce_x(c):
        copies = []
        for j in range(1, NX):
            x, k = (mx + j) % NX, 4 * c + j
            to = x * NY + my
            copies.append(remote(part.at[group_rows(x), held[c]], rx.at[j - 1, :, held[c]], sx.at[k], rxs.at[k], to, peer))
            if c == 0:
                copies.append(remote(npart, nrx.at[j - 1], sn.at[j], rn.at[j], to, peer))
        flying[c] = started(copies)

    def reduce_y(c):
        landed(c)
        total = part[group_rows(mx), held[c]].astype(F32)
        for j in range(NX - 1):
            total += rx[j, :, held[c]].astype(F32)
        px[:, held[c]] = total.astype(BF16)
        if c == 0:
            npx[...] = npart[...] + nrx[0] + nrx[1] + nrx[2]
        copies = []
        for j in range(1, NY):
            y, k = (my + j) % NY, 4 * c + j
            to = mx * NY + y
            copies.append(remote(px.at[rank_rows(y), held[c]], ry.at[j - 1, :, held[c]], sy.at[k], rys.at[k], to, peer))
            if c == 0:
                copies.append(remote(npx, nry.at[j - 1], sm.at[j], rm.at[j], to, peer))
        flying[c] = started(copies)

    def gather_y(c):
        landed(c)
        total = px[rank_rows(my), held[c]].astype(F32)
        for j in range(NY - 1):
            total += ry[j, :, held[c]].astype(F32)
        x_ref[mine, held[c]] = total.astype(BF16)
        if c == 0:
            n_ref[...] = npx[...] + nry[0] + nry[1] + nry[2]
        rows = x_ref.at[mine, held[c]]
        flying[c] = started(
            [
                remote(rows, rows, sg.at[4 * c + j], rg.at[4 * c + j], mx * NY + (my + j) % NY, peer)
                for j in range(1, NY)
            ]
        )

    def gather_x(c):
        landed(c)
        rows = x_ref.at[group_rows(mx), held[c]]
        flying[c] = started(
            [
                remote(rows, rows, sh.at[4 * c + j], rh.at[4 * c + j], ((mx + j) % NX) * NY + my, peer)
                for j in range(1, NX)
            ]
        )

    for copy in b_copies:
        copy.wait()
    bf = bf_ref[...]
    part[:, ALL + TOKENS : ALL + 2 * TOKENS] = (dot(bf, h, NT) * rs).astype(BF16)
    part[:, ALL + 2 * TOKENS : XW] = (dot(bf, q_ref[...], NT) * rs).astype(BF16)
    reduce_x(0)
    for copy in a_copies:
        copy.wait()
    af = af_ref[...]
    lower, _ = block_masks()

    def squares(at):
        other = bf_ref[at : at + ALL // 2, :]
        mask = lower[:, at : at + ALL // 2]
        products = jnp.where(mask, dot(af, other, NT) * rs, dot(bf, other, NT) * (1.0 / RANK))
        part[:, at : at + ALL // 2] = products.astype(BF16)

    part[:, ALL : ALL + TOKENS] = dot(af, h, NT).astype(BF16)
    squares(ALL // 2)
    reduce_x(1)
    squares(0)
    reduce_x(2)
    reduce_y(0)
    reduce_y(1)
    gather_y(0)
    reduce_y(2)
    gather_y(1)
    gather_x(0)
    gather_y(2)
    gather_x(1)
    gather_x(2)
    for c in range(len(CHUNKS)):
        landed(c)


def products(bits, h, q, gain, a, b):
    dma = pltpu.SemaphoreType.DMA
    group = NY * RANK
    return pl.pallas_call(
        products_kernel,
        out_shape=(
            jax.ShapeDtypeStruct((1,), jnp.int32),
            jax.ShapeDtypeStruct((ALL, XW), BF16),
            jax.ShapeDtypeStruct((8, TOKENS), F32),
            jax.ShapeDtypeStruct((ALL, SLICE), BF16),
            jax.ShapeDtypeStruct((ALL, SLICE), BF16),
        ),
        in_specs=[SMEM] + [pl.BlockSpec(memory_space=pl.ANY)] * 5,
        out_specs=(SMEM,) + (VMEM,) * 4,
        scratch_shapes=[
            pltpu.VMEM((TOKENS, SLICE), BF16),
            pltpu.VMEM((TOKENS, SLICE), BF16),
            pltpu.VMEM((1, WIDTH), F32),
            pltpu.VMEM((RANK, WIDTH), BF16),
            pltpu.VMEM((RANK, WIDTH), BF16),
            dma((5,)),
            pltpu.VMEM((RANK, WIDTH), BF16),
            pltpu.VMEM((ALL, XW), BF16),
            pltpu.VMEM((NX - 1, group, XW), BF16),
            pltpu.VMEM((group, XW), BF16),
            pltpu.VMEM((NY - 1, RANK, XW), BF16),
            pltpu.VMEM((8, TOKENS), F32),
            pltpu.VMEM((NX - 1, 8, TOKENS), F32),
            pltpu.VMEM((8, TOKENS), F32),
            pltpu.VMEM((NY - 1, 8, TOKENS), F32),
        ]
        + [dma((SECTIONS,))] * 4
        + [dma((4 * len(CHUNKS),))] * 8
        + [dma((4,))] * 4,
        compiler_params=pltpu.CompilerParams(collective_id=0, has_side_effects=True, vmem_limit_bytes=LIMIT),
        name="products",
    )(bits, h, q, gain, a, b)


def rows_of(s):
    return slice(RANK * s, RANK * s + RANK)


def forward(x_ref, n_ref, xt, lat, wp, rms):
    xt[...] = x_ref[:, 0:ALL].astype(F32).T.astype(BF16)
    norm = n_ref[0:1, :]
    for s in range(SECTIONS):
        rows = rows_of(s)
        u = x_ref[rows, ALL : ALL + TOKENS].astype(F32)
        w = x_ref[rows, ALL + TOKENS : ALL + 2 * TOKENS].astype(F32)
        if s > 0:
            before = lat[0 : RANK * s, :]
            u += dot(x_ref[rows, 0 : RANK * s], before)
            w += dot(xt[rows, 0 : RANK * s], before)
        r = lax.rsqrt(jnp.maximum(norm, 0.0) * (1.0 / WIDTH) + 1e-5)
        latent = (u * r).astype(BF16)
        lat[rows, :] = latent
        after = w + dot(xt[rows, rows], latent)
        norm += jnp.sum(latent.astype(F32) * (w + after), axis=0, keepdims=True)
        wp[rows, :] = after
        rms[s : s + 1, :] = r


def backward(x_ref, xt, lat, scaled_inner, cl, wp, rms):
    carry = jnp.zeros((1, TOKENS), F32)
    for s in reversed(range(SECTIONS)):
        rows = rows_of(s)
        inner = x_ref[rows, ALL + 2 * TOKENS : XW].astype(F32) - carry * wp[rows, :]
        if s < SECTIONS - 1:
            later = RANK * (s + 1)
            inner += dot(xt[rows, later:ALL], scaled_inner[later:ALL, :])
            inner -= dot(x_ref[rows, later:ALL], cl[later:ALL, :])
        r = rms[s : s + 1, :]
        latent = lat[rows, :].astype(F32)
        scaled_inner[rows, :] = (r * inner).astype(BF16)
        cl[rows, :] = (carry * latent).astype(BF16)
        carry += r * r * (jnp.sum(latent * inner, axis=0, keepdims=True) * (1.0 / WIDTH))


def down_gradient(af_ref, bf_ref, h_ref, lat, scaled_inner, gd_ref):
    lower, _ = block_masks()
    ri = scaled_inner[...]
    mixed = jnp.where(lower, dot(ri, lat[...], NT), 0.0).astype(BF16)
    down = dot(ri, h_ref[...]) + dot(mixed, bf_ref[...]) * RANK**-0.5
    gd_ref[...] = (down * WIDTH**-0.5).astype(BF16)


def up_gradient(af_ref, bf_ref, h_ref, q_ref, lat, scaled_inner, cl, gu_ref):
    _, upper = block_masks()
    rs = RANK**-0.5
    ls, ri, cls = lat[...], scaled_inner[...], cl[...]
    mixed = jnp.where(upper, dot(ls, cls, NT), dot(cls, ls, NT)).astype(BF16)
    up = dot(ls, q_ref[...]) - dot(cls, h_ref[...]) - dot(mixed, bf_ref[...]) * rs
    up += dot(jnp.where(upper, dot(ls, ri, NT), 0.0).astype(BF16), af_ref[...])
    gu_ref[...] = (up * rs).astype(BF16)


CHAIN_SCRATCH = [
    pltpu.VMEM((ALL, SLICE), BF16),
    pltpu.VMEM((ALL, SLICE), BF16),
    pltpu.VMEM((ALL, ALL), BF16),
    pltpu.VMEM((ALL, TOKENS), BF16),
    pltpu.VMEM((ALL, TOKENS), BF16),
    pltpu.VMEM((ALL, TOKENS), BF16),
    pltpu.VMEM((ALL, TOKENS), F32),
    pltpu.VMEM((SECTIONS, TOKENS), F32),
]


def adam(param, first, second, grad):
    first_new = 0.9 * first.astype(F32) + 0.1 * grad
    second_new = 0.999 * second.astype(F32) + 0.001 * grad * grad
    corr_one = 1.0 - 0.9**ADAM_STEP
    corr_two = 1.0 - 0.999**ADAM_STEP
    update = 0.05 * (first_new / corr_one) / (jnp.sqrt(second_new / corr_two) + 1e-08)
    return param.astype(F32) - update, first_new, second_new


def make_update(bits, number):
    zbits = tuple(b for b in bits if b not in (0, 4))
    group = 1 << len(zbits)
    offsets = [sum(1 << b for i, b in enumerate(zbits) if m >> i & 1) for m in range(group)]
    half_width = WIDTH // 2
    rows_each = 3 * RANK
    turn = half_width if len(zbits) == 0 or zbits == (1,) else half_width // 2

    def kernel(x_ref, n_ref, af_ref, bf_ref, h_ref, q_ref, g_ref, *rest):
        held, out, rest = rest[:6], rest[6], rest[7:]
        gd, gu, xt, lat, scaled_inner, cl, wp, rms = rest[:8]
        state, other, half, gdf, gup, sl, so, ro, sd, rd, su, ru, sj, rj = rest[8:22]
        rest = rest[22:]
        me, peer = lax.axis_index("section"), lax.axis_index("peer")
        core, far = peer % 2, peer // 16
        rank = sum(((peer // (1 << b)) % 2) * (1 << i) for i, b in enumerate(zbits)) if zbits else 0
        keeper = me // 8
        place = pl.ds(pl.multiple_of((me % 8) * SLICE, SLICE), SLICE)
        foreign = (core + keeper) % 2
        slot = foreign * 8 + me % 8

        loads = [pltpu.make_async_copy(held[k], state.at[k], sl.at[k]) for k in range(6)]
        for load in loads:
            load.start()
        barrier = pltpu.get_barrier_semaphore()

        def signal(section, to):
            pl.semaphore_signal(barrier, inc=1, device_id=(section, to), device_id_type=MESH)

        for k in range(8):
            source = core * 8 + k
            signal(source, peer + 1 - 2 * core)

            @pl.when(source != me)
            def _():
                signal(source, peer)

        partners = [1, 16] + offsets[1:]
        for offset in partners:
            signal(me, peer ^ offset)
        forward(x_ref, n_ref, xt, lat, wp, rms)
        pl.semaphore_wait(barrier, SECTIONS - 1 + foreign + len(partners))
        for load in loads:
            load.wait()
        theirs = pl.ds(pl.multiple_of((1 - core) * half_width, half_width), half_width)
        swaps = [remote(state.at[k, :, theirs], other.at[k], so.at[k], ro.at[k], me, peer ^ 1) for k in range(6)]
        for copy in swaps:
            copy.start()
        backward(x_ref, xt, lat, scaled_inner, cl, wp, rms)

        def gradient_copy(src, dst, send, recv, j):
            to = (me + j) % SECTIONS
            rows = pl.ds(pl.multiple_of(to * RANK, RANK), RANK)
            return remote(
                src.at[rows], dst.at[foreign, :, place], send.at[j], recv.at[slot], to, peer - core + keeper
            )

        def scatter(src, dst, send, recv):
            for j in range(1, SECTIONS):
                gradient_copy(src, dst, send, recv, j).start()

            @pl.when(foreign == 1)
            def _():
                gradient_copy(src, dst, send, recv, 0).start()

            @pl.when(foreign == 0)
            def _():
                dst[0, :, place] = src[pl.ds(pl.multiple_of(me * RANK, RANK), RANK), :]

        def scattered(src, dst, send, recv):
            for j in range(1, SECTIONS):
                gradient_copy(src, dst, send, recv, j).wait_send()

            @pl.when(foreign == 1)
            def _():
                gradient_copy(src, dst, send, recv, 0).wait_send()

        down_gradient(af_ref, bf_ref, h_ref, lat, scaled_inner, gd)
        scatter(gd, gdf, sd, rd)
        up_gradient(af_ref, bf_ref, h_ref, q_ref, lat, scaled_inner, cl, gu)
        scatter(gu, gup, su, ru)
        for copy in swaps:
            copy.wait()

        def adam_pairs(dst, src, recv, which, gain):
            def step(i, _):
                k = (me + i) % 8
                source = core * 8 + k
                cols = pl.ds(pl.multiple_of(source * SLICE, SLICE), SLICE)
                here = pl.ds(pl.multiple_of(k * SLICE, SLICE), SLICE)

                @pl.when(source != me)
                def _():
                    remote(src.at[0:RANK], dst.at[0, :, here], sd.at[0], recv.at[k], me, peer ^ 1).wait_recv()

                remote(src.at[0:RANK], dst.at[1, :, here], sd.at[0], recv.at[8 + k], me, peer ^ 1).wait_recv()
                grads = [dst[m, :, here].astype(F32) for m in range(2)]
                if gain:
                    grads = [grad * g_ref[:, cols] for grad in grads]
                mine = adam(*[state[2 * m + which, :, cols] for m in range(3)], grads[0])
                pair = adam(*[other[2 * m + which, :, here] for m in range(3)], grads[1])
                for m in range(3):
                    at = rows_each * which + RANK * m
                    half[at : at + RANK, here] = ((mine[m] + pair[m]) * 0.5).astype(BF16)
                return 0

            lax.fori_loop(0, 8, step, 0)

        def mean(*values):
            total = values[0].astype(F32)
            for value in values[1:]:
                total += value.astype(F32)
            return (total * (1.0 / len(values))).astype(BF16)

        def cols_at(at, width):
            return pl.ds(pl.multiple_of(at, 128), width)

        base = core * half_width
        pending = []
        count = iter(range(64))

        def send(src, dst, offset):
            k = next(count)
            copy = remote(src, dst, sj.at[k], rj.at[k], me, peer ^ offset)
            copy.start()
            return copy

        def join(rows, at, width):
            there = out.at[rows, cols_at(base + at, width)]
            pending.append(send(there, there, 1))

        down, up = slice(0, rows_each), slice(rows_each, 2 * rows_each)

        def only_y(rows, at, width, land):
            copy = send(half.at[rows, at : at + width], land, 16)
            yield
            copy.wait()
            out[rows, cols_at(base + at, width)] = mean(half[rows, at : at + width], land[...])
            join(rows, at, width)
            yield

        def z_first(rows, at, width, land_z, acc, land_y):
            part = width // group
            copies = [
                send(half.at[rows, cols_at(at + (rank ^ m) * part, part)], land_z.at[m - 1], offsets[m])
                for m in range(1, group)
            ]
            yield
            for copy in copies:
                copy.wait()
            acc[...] = mean(half[rows, cols_at(at + rank * part, part)], *[land_z[m] for m in range(group - 1)])
            copy = send(acc, land_y, 16)
            yield
            copy.wait()
            here = cols_at(base + at + rank * part, part)
            out[rows, here] = mean(acc[...], land_y[...])
            copies = [send(out.at[rows, here], out.at[rows, here], offsets[m]) for m in range(1, group)]
            yield
            for copy in copies:
                copy.wait()
            join(rows, at, width)
            yield

        def y_first(rows, at, width, land_y, acc, land_z):
            wide = width // 2
            part = wide // group
            copy = send(half.at[rows, cols_at(at + (1 - far) * wide, wide)], land_y, 16)
            yield
            copy.wait()
            acc[...] = mean(half[rows, cols_at(at + far * wide, wide)], land_y[...])
            whole = cols_at(base + at + far * wide, wide)
            if group == 2:
                copies = [send(acc, land_z.at[0], offsets[1])]
            else:
                copies = [
                    send(acc.at[:, cols_at((rank ^ m) * part, part)], land_z.at[m - 1], offsets[m])
                    for m in range(1, group)
                ]
            yield
            for copy in copies:
                copy.wait()
            if group == 2:
                out[rows, whole] = mean(acc[...], land_z[0])
            else:
                here = cols_at(base + at + far * wide + rank * part, part)
                own = acc[:, cols_at(rank * part, part)]
                out[rows, here] = mean(own, *[land_z[m] for m in range(group - 1)])
                copies = [send(out.at[rows, here], out.at[rows, here], offsets[m]) for m in range(1, group)]
                yield
                for copy in copies:
                    copy.wait()
            copy = send(out.at[rows, whole], out.at[rows, whole], 16)
            yield
            copy.wait()
            join(rows, at, width)
            yield

        if not zbits:
            quarter = half_width // 2
            first = [only_y(down, 0, quarter, rest[0]), only_y(down, quarter, quarter, rest[1])]
            second = [only_y(up, 0, quarter, rest[2]), only_y(up, quarter, quarter, rest[3])]
        else:
            first = [z_first(down, 0, half_width, *rest[0:3])]
            second = [z_first(up, 0, turn, *rest[3:6])]
            if turn < half_width:
                second = [y_first(up, turn, half_width - turn, *rest[6:9])] + second

        adam_pairs(gdf, gd, rd, 0, True)
        if zbits:
            for chunk in first:
                next(chunk)
        adam_pairs(gup, gu, ru, 1, False)
        for chunk in second if zbits else first + second:
            next(chunk)
        chunks = first + second
        while chunks:
            chunks = [chunk for chunk in chunks if next(chunk, "end") != "end"]
        for copy in pending:
            copy.wait()
        scattered(gd, gdf, sd, rd)
        scattered(gu, gup, su, ru)

    dma = pltpu.SemaphoreType.DMA

    def blocks(*shape):
        return pltpu.VMEM(shape, BF16)

    scratch = CHAIN_SCRATCH + [
        blocks(6, RANK, WIDTH),
        blocks(6, RANK, half_width),
        blocks(6 * RANK, half_width),
        blocks(2, RANK, half_width),
        blocks(2, RANK, half_width),
    ]
    scratch += [dma((6,))] * 3 + [dma((SECTIONS,))] * 4 + [dma((32,))] * 2
    if not zbits:
        scratch += [blocks(rows_each, half_width // 2)] * 4
    else:
        for width in (half_width, turn):
            part = width // group
            scratch += [blocks(group - 1, rows_each, part), blocks(rows_each, part), blocks(rows_each, part)]
        if turn < half_width:
            wide = (half_width - turn) // 2
            part = wide if group == 2 else wide // group
            scratch += [blocks(rows_each, wide), blocks(rows_each, wide), blocks(group - 1, rows_each, part)]

    def update(*operands):
        return pl.pallas_call(
            kernel,
            out_shape=jax.ShapeDtypeStruct((6 * RANK, WIDTH), BF16),
            in_specs=[VMEM] * 7 + [pl.BlockSpec(memory_space=pl.ANY)] * 6,
            out_specs=VMEM,
            scratch_shapes=scratch,
            compiler_params=pltpu.CompilerParams(
                collective_id=1 + number, has_side_effects=True, vmem_limit_bytes=LIMIT
            ),
            name=f"update_{number}",
        )(*operands)

    return update


CASES = [(0, 4), (0, 1, 4), (0, 2, 4), (0, 1, 2, 4), (0, 3, 4), (0, 1, 3, 4), (0, 2, 3, 4)]


def on_device(hidden_in, cotangent, norm_gain, *rest):
    *state, round_bits = rest
    state = [
        jnp.swapaxes(array[0, 0], 0, 1) if number % 2 == 0 else array[0, 0] for number, array in enumerate(state)
    ]
    a, b = state[:2]
    h, q = hidden_in[0], cotangent[0]
    case, x, n, af, bf = products(round_bits, h, q, norm_gain, a, b)
    branches = [make_update(bits, i) for i, bits in enumerate(CASES)]
    out = lax.switch(case[0], branches, x, n, af, bf, h, q, norm_gain, *state)
    parts = [out[RANK * k : RANK * k + RANK] for k in (0, 3, 1, 4, 2, 5)]
    return tuple((jnp.swapaxes(p, 0, 1) if k % 2 == 0 else p)[None, None] for k, p in enumerate(parts))


def solution(mesh):
    held = P("section", "peer", None, None)
    return jax.shard_map(
        on_device,
        mesh=mesh,
        in_specs=(P("peer", None, "section"), P("peer", None, "section"), P("section", None)) + (held,) * 6 + (P(),),
        out_specs=(held,) * 6,
        check_vma=False,
    )
```

```python
import jax
import jax.numpy as jnp
from jax import lax
from jax.experimental import pallas as pl
from jax.experimental.pallas import tpu as pltpu
from jax.sharding import PartitionSpec as P

ADAM_STEP = 100
MESH = pl.DeviceIdType.MESH
F32, BF16 = jnp.float32, jnp.bfloat16
SECTIONS, NX, NY = 16, 4, 4
RANK, WIDTH, TOKENS = 32, 4096, 128
SLICE = WIDTH // SECTIONS
ALL = SECTIONS * RANK
XW = ALL + 3 * TOKENS
SQ, WS, ZS = TOKENS, TOKENS + ALL, 2 * TOKENS + ALL
VMEM = pl.BlockSpec(memory_space=pltpu.VMEM)
SMEM = pl.BlockSpec(memory_space=pltpu.SMEM)
LIMIT = 48 << 20

NN = (((1,), (0,)), ((), ()))
NT = (((1,), (1,)), ((), ()))


def dot(a, b, dims=NN):
    return lax.dot_general(a, b, dims, preferred_element_type=F32)


def block_masks():
    row = lax.broadcasted_iota(jnp.int32, (ALL, ALL), 0) // RANK
    col = lax.broadcasted_iota(jnp.int32, (ALL, ALL), 1) // RANK
    return row > col, row < col


def remote(src, dst, send, recv, section, peer):
    return pltpu.make_async_remote_copy(
        src_ref=src, dst_ref=dst, send_sem=send, recv_sem=recv, device_id=(section, peer), device_id_type=MESH
    )


CHUNKS = ((WS, 2 * TOKENS), (0, SQ + ALL // 2), (SQ + ALL // 2, ALL // 2))


def products_kernel(
    bits_hbm, h_hbm, q_hbm, g_hbm, a_hbm, b_hbm, case_ref, x_ref, af_ref, bf_ref, xt, lat, wp, rms,
    bits_ref, h_ref, q_ref, g_ref, a_ref, b_ref, loaded, n_ref, scaled, part, rx, px, ry, npart, nrx, npx, nry, sa, ra, sb, rb, sx, rxs, sy, rys, sg, rg, sh, rh, sn, rn, sm, rm,
):
    me, peer = lax.axis_index("section"), lax.axis_index("peer")
    mx, my = me // NY, me % NY

    operands = [(a_hbm, a_ref), (g_hbm, g_ref), (b_hbm, b_ref), (h_hbm, h_ref), (q_hbm, q_ref), (bits_hbm, bits_ref)]
    loads = [pltpu.make_async_copy(src, dst, loaded.at[k]) for k, (src, dst) in enumerate(operands)]
    for load in loads:
        load.start()
    barrier = pltpu.get_barrier_semaphore()
    for j in range(1, SECTIONS):
        pl.semaphore_signal(barrier, inc=1, device_id=((me + j) % SECTIONS, peer), device_id_type=MESH)
    for load in loads:
        load.wait()
    case_ref[0] = sum(
        jnp.maximum(
            jnp.maximum((bits_ref[0] == bit).astype(jnp.int32), (bits_ref[1] == bit).astype(jnp.int32)),
            jnp.maximum((bits_ref[2] == bit).astype(jnp.int32), (bits_ref[3] == bit).astype(jnp.int32)),
        )
        << (bit - 1)
        for bit in (1, 2, 3)
    )
    scaled[...] = (a_ref[...].astype(F32) * (g_ref[...] * WIDTH**-0.5)).astype(BF16)
    pl.semaphore_wait(barrier, SECTIONS - 1)

    mine = pl.ds(pl.multiple_of(me * RANK, RANK), RANK)

    def scatter(src, dst, send, recv):
        copies = []
        for j in range(1, SECTIONS):
            to = (me + j) % SECTIONS
            cols = pl.ds(pl.multiple_of(to * SLICE, SLICE), SLICE)
            copies.append(remote(src.at[:, cols], dst.at[mine], send.at[j], recv.at[j], to, peer))
        for copy in copies:
            copy.start()
        return copies

    b_copies = scatter(b_ref, bf_ref, sb, rb)
    a_copies = scatter(scaled, af_ref, sa, ra)
    cols = pl.ds(pl.multiple_of(me * SLICE, SLICE), SLICE)
    af_ref[mine, :] = scaled[:, cols]
    bf_ref[mine, :] = b_ref[:, cols]
    h = h_ref[...]
    square = h.astype(F32) * h.astype(F32)
    high = square.astype(BF16)
    low = (square - high.astype(F32)).astype(BF16)
    ones = jnp.ones((8, SLICE), BF16)
    npart[...] = dot(ones, high, NT) + dot(ones, low, NT)
    rs = RANK**-0.5

    def group_rows(x):
        return pl.ds(pl.multiple_of(x * NY * RANK, NY * RANK), NY * RANK)

    def rank_rows(y):
        return pl.ds(pl.multiple_of(y * RANK, RANK), RANK)

    held = [pl.ds(at, width) for at, width in CHUNKS]
    flying = [None] * len(CHUNKS)

    def started(copies):
        for copy in copies:
            copy.start()
        return copies

    def landed(c):
        for copy in flying[c]:
            copy.wait()

    def reduce_x(c):
        copies = []
        for j in range(1, NX):
            x, k = (mx + j) % NX, 4 * c + j
            to = x * NY + my
            copies.append(remote(part.at[group_rows(x), held[c]], rx.at[j - 1, :, held[c]], sx.at[k], rxs.at[k], to, peer))
            if c == 0:
                copies.append(remote(npart, nrx.at[j - 1], sn.at[j], rn.at[j], to, peer))
        flying[c] = started(copies)

    def reduce_y(c):
        landed(c)
        total = part[group_rows(mx), held[c]].astype(F32)
        for j in range(NX - 1):
            total += rx[j, :, held[c]].astype(F32)
        px[:, held[c]] = total.astype(BF16)
        if c == 0:
            npx[...] = npart[...] + nrx[0] + nrx[1] + nrx[2]
        copies = []
        for j in range(1, NY):
            y, k = (my + j) % NY, 4 * c + j
            to = mx * NY + y
            copies.append(remote(px.at[rank_rows(y), held[c]], ry.at[j - 1, :, held[c]], sy.at[k], rys.at[k], to, peer))
            if c == 0:
                copies.append(remote(npx, nry.at[j - 1], sm.at[j], rm.at[j], to, peer))
        flying[c] = started(copies)

    def gather_y(c):
        landed(c)
        total = px[rank_rows(my), held[c]].astype(F32)
        for j in range(NY - 1):
            total += ry[j, :, held[c]].astype(F32)
        x_ref[mine, held[c]] = total.astype(BF16)
        if c == 0:
            n_ref[...] = npx[...] + nry[0] + nry[1] + nry[2]
        rows = x_ref.at[mine, held[c]]
        flying[c] = started(
            [
                remote(rows, rows, sg.at[4 * c + j], rg.at[4 * c + j], mx * NY + (my + j) % NY, peer)
                for j in range(1, NY)
            ]
        )

    def gather_x(c):
        landed(c)
        rows = x_ref.at[group_rows(mx), held[c]]
        flying[c] = started(
            [
                remote(rows, rows, sh.at[4 * c + j], rh.at[4 * c + j], ((mx + j) % NX) * NY + my, peer)
                for j in range(1, NX)
            ]
        )

    for copy in b_copies:
        copy.wait()
    bf = bf_ref[...]
    part[:, WS:ZS] = (dot(bf, h, NT) * rs).astype(BF16)
    part[:, ZS:XW] = (dot(bf, q_ref[...], NT) * rs).astype(BF16)
    reduce_x(0)
    for copy in a_copies:
        copy.wait()
    af = af_ref[...]
    lower, _ = block_masks()

    def squares(at):
        other = bf_ref[at : at + ALL // 2, :]
        mask = lower[:, at : at + ALL // 2]
        products = jnp.where(mask, dot(af, other, NT) * rs, dot(bf, other, NT) * (1.0 / RANK))
        part[:, SQ + at : SQ + at + ALL // 2] = products.astype(BF16)

    part[:, 0:SQ] = dot(af, h, NT).astype(BF16)
    squares(0)
    reduce_x(1)
    squares(ALL // 2)
    reduce_x(2)
    reduce_y(0)
    reduce_y(1)
    gather_y(0)
    reduce_y(2)
    gather_y(1)
    gather_x(0)
    gather_y(2)
    gather_x(1)
    gather_x(2)
    landed(0)
    landed(1)
    norm = forward(range(SECTIONS // 2), n_ref[0:1, :], x_ref, xt, lat, wp, rms)
    landed(2)
    forward(range(SECTIONS // 2, SECTIONS), norm, x_ref, xt, lat, wp, rms)


def products(bits, h, q, gain, a, b):
    dma = pltpu.SemaphoreType.DMA
    group = NY * RANK
    return pl.pallas_call(
        products_kernel,
        out_shape=(
            jax.ShapeDtypeStruct((1,), jnp.int32),
            jax.ShapeDtypeStruct((ALL, XW), BF16),
            jax.ShapeDtypeStruct((ALL, SLICE), BF16),
            jax.ShapeDtypeStruct((ALL, SLICE), BF16),
            jax.ShapeDtypeStruct((ALL, ALL), BF16),
            jax.ShapeDtypeStruct((ALL, TOKENS), BF16),
            jax.ShapeDtypeStruct((ALL, TOKENS), F32),
            jax.ShapeDtypeStruct((SECTIONS, TOKENS), F32),
        ),
        in_specs=[pl.BlockSpec(memory_space=pl.ANY)] * 6,
        out_specs=(SMEM,) + (VMEM,) * 7,
        scratch_shapes=[
            pltpu.SMEM((4,), jnp.int32),
            pltpu.VMEM((TOKENS, SLICE), BF16),
            pltpu.VMEM((TOKENS, SLICE), BF16),
            pltpu.VMEM((1, WIDTH), F32),
            pltpu.VMEM((RANK, WIDTH), BF16),
            pltpu.VMEM((RANK, WIDTH), BF16),
            dma((6,)),
            pltpu.VMEM((8, TOKENS), F32),
            pltpu.VMEM((RANK, WIDTH), BF16),
            pltpu.VMEM((ALL, XW), BF16),
            pltpu.VMEM((NX - 1, group, XW), BF16),
            pltpu.VMEM((group, XW), BF16),
            pltpu.VMEM((NY - 1, RANK, XW), BF16),
            pltpu.VMEM((8, TOKENS), F32),
            pltpu.VMEM((NX - 1, 8, TOKENS), F32),
            pltpu.VMEM((8, TOKENS), F32),
            pltpu.VMEM((NY - 1, 8, TOKENS), F32),
        ]
        + [dma((SECTIONS,))] * 4
        + [dma((4 * len(CHUNKS),))] * 8
        + [dma((4,))] * 4,
        compiler_params=pltpu.CompilerParams(collective_id=0, has_side_effects=True, vmem_limit_bytes=LIMIT),
        name="products",
    )(bits, h, q, gain, a, b)


def rows_of(s):
    return slice(RANK * s, RANK * s + RANK)


def forward(sections, norm, x_ref, xt, lat, wp, rms):
    half = slice(RANK * sections[0], RANK * sections[-1] + RANK)
    xt[half, :] = x_ref[:, SQ + half.start : SQ + half.stop].astype(F32).T.astype(BF16)
    for s in sections:
        rows = rows_of(s)
        u = x_ref[rows, 0:SQ].astype(F32)
        w = x_ref[rows, WS:ZS].astype(F32)
        if s > 0:
            before = lat[0 : RANK * s, :]
            u += dot(x_ref[rows, SQ : SQ + RANK * s], before)
            w += dot(xt[rows, 0 : RANK * s], before)
        r = lax.rsqrt(jnp.maximum(norm, 0.0) * (1.0 / WIDTH) + 1e-5)
        latent = (u * r).astype(BF16)
        lat[rows, :] = latent
        after = w + dot(xt[rows, rows], latent)
        norm += jnp.sum(latent.astype(F32) * (w + after), axis=0, keepdims=True)
        wp[rows, :] = after
        rms[s : s + 1, :] = r
    return norm


def backward(x_ref, xt, lat, scaled_inner, cl, wp, rms):
    carry = jnp.zeros((1, TOKENS), F32)
    for s in reversed(range(SECTIONS)):
        rows = rows_of(s)
        inner = x_ref[rows, ZS:XW].astype(F32) - carry * wp[rows, :]
        if s < SECTIONS - 1:
            later = RANK * (s + 1)
            inner += dot(xt[rows, later:ALL], scaled_inner[later:ALL, :])
            inner -= dot(x_ref[rows, SQ + later : SQ + ALL], cl[later:ALL, :])
        r = rms[s : s + 1, :]
        latent = lat[rows, :].astype(F32)
        scaled_inner[rows, :] = (r * inner).astype(BF16)
        cl[rows, :] = (carry * latent).astype(BF16)
        carry += r * r * (jnp.sum(latent * inner, axis=0, keepdims=True) * (1.0 / WIDTH))


def down_gradient(af_ref, bf_ref, h_ref, lat, scaled_inner, gd_ref):
    lower, _ = block_masks()
    ri = scaled_inner[...]
    mixed = jnp.where(lower, dot(ri, lat[...], NT), 0.0).astype(BF16)
    down = dot(ri, h_ref[...]) + dot(mixed, bf_ref[...]) * RANK**-0.5
    gd_ref[...] = (down * WIDTH**-0.5).astype(BF16)


def up_gradient(af_ref, bf_ref, h_ref, q_ref, lat, scaled_inner, cl, gu_ref):
    _, upper = block_masks()
    rs = RANK**-0.5
    ls, ri, cls = lat[...], scaled_inner[...], cl[...]
    mixed = jnp.where(upper, dot(ls, cls, NT), dot(cls, ls, NT)).astype(BF16)
    up = dot(ls, q_ref[...]) - dot(cls, h_ref[...]) - dot(mixed, bf_ref[...]) * rs
    up += dot(jnp.where(upper, dot(ls, ri, NT), 0.0).astype(BF16), af_ref[...])
    gu_ref[...] = (up * rs).astype(BF16)


CHAIN_SCRATCH = [
    pltpu.VMEM((ALL, SLICE), BF16),
    pltpu.VMEM((ALL, SLICE), BF16),
    pltpu.VMEM((ALL, TOKENS), BF16),
    pltpu.VMEM((ALL, TOKENS), BF16),
]


def adam(param, first, second, grad):
    first_new = 0.9 * first.astype(F32) + 0.1 * grad
    second_new = 0.999 * second.astype(F32) + 0.001 * grad * grad
    corr_one = 1.0 - 0.9**ADAM_STEP
    corr_two = 1.0 - 0.999**ADAM_STEP
    update = 0.05 * (first_new / corr_one) / (jnp.sqrt(second_new / corr_two) + 1e-08)
    return param.astype(F32) - update, first_new, second_new


def make_update(bits, number):
    zbits = tuple(b for b in bits if b not in (0, 4))
    group = 1 << len(zbits)
    offsets = [sum(1 << b for i, b in enumerate(zbits) if m >> i & 1) for m in range(group)]
    half_width = WIDTH // 2
    rows_each = 3 * RANK
    turn = {(): half_width, (2,): 512, (3,): 512, (1, 2): half_width}.get(zbits, half_width // 2)

    def kernel(x_ref, af_ref, bf_ref, xt, lat, wp, rms, h_ref, q_ref, g_ref, *rest):
        held, outs, rest = rest[:6], rest[6:8], rest[8:]
        gd, gu, scaled_inner, cl = rest[:4]
        state, other, half, gdf, gup, sl, so, ro, sd, rd, su, ru, sj, rj = rest[4:18]
        rest = rest[18:]
        me, peer = lax.axis_index("section"), lax.axis_index("peer")
        core, far = peer % 2, peer // 16
        rank = sum(((peer // (1 << b)) % 2) * (1 << i) for i, b in enumerate(zbits)) if zbits else 0
        keeper = me // 8
        place = pl.ds(pl.multiple_of((me % 8) * SLICE, SLICE), SLICE)
        foreign = (core + keeper) % 2
        slot = foreign * 8 + me % 8

        loads = [pltpu.make_async_copy(held[k], state.at[k], sl.at[k]) for k in range(6)]
        for load in loads:
            load.start()
        barrier = pltpu.get_barrier_semaphore()

        def signal(section, to):
            pl.semaphore_signal(barrier, inc=1, device_id=(section, to), device_id_type=MESH)

        for k in range(8):
            source = core * 8 + k
            signal(source, peer + 1 - 2 * core)

            @pl.when(source != me)
            def _():
                signal(source, peer)

        partners = [1, 16] + offsets[1:]
        for offset in partners:
            signal(me, peer ^ offset)
        backward(x_ref, xt, lat, scaled_inner, cl, wp, rms)
        down_gradient(af_ref, bf_ref, h_ref, lat, scaled_inner, gd)
        pl.semaphore_wait(barrier, SECTIONS - 1 + foreign + len(partners))

        def gradient_copy(src, dst, send, recv, j):
            to = (me + j) % SECTIONS
            rows = pl.ds(pl.multiple_of(to * RANK, RANK), RANK)
            return remote(
                src.at[rows], dst.at[foreign, :, place], send.at[j], recv.at[slot], to, peer - core + keeper
            )

        def scatter(src, dst, send, recv):
            for j in range(1, SECTIONS):
                gradient_copy(src, dst, send, recv, j).start()

            @pl.when(foreign == 1)
            def _():
                gradient_copy(src, dst, send, recv, 0).start()

            @pl.when(foreign == 0)
            def _():
                dst[0, :, place] = src[pl.ds(pl.multiple_of(me * RANK, RANK), RANK), :]

        def scattered(src, dst, send, recv):
            for j in range(1, SECTIONS):
                gradient_copy(src, dst, send, recv, j).wait_send()

            @pl.when(foreign == 1)
            def _():
                gradient_copy(src, dst, send, recv, 0).wait_send()

        scatter(gd, gdf, sd, rd)
        for load in loads:
            load.wait()
        theirs = pl.ds(pl.multiple_of((1 - core) * half_width, half_width), half_width)
        swaps = [remote(state.at[k, :, theirs], other.at[k], so.at[k], ro.at[k], me, peer ^ 1) for k in range(6)]
        for copy in swaps:
            copy.start()
        up_gradient(af_ref, bf_ref, h_ref, q_ref, lat, scaled_inner, cl, gu)
        scatter(gu, gup, su, ru)
        for copy in swaps:
            copy.wait()

        def adam_pairs(dst, src, recv, which, gain):
            def step(i, _):
                k = (me + i) % 8
                source = core * 8 + k
                cols = pl.ds(pl.multiple_of(source * SLICE, SLICE), SLICE)
                here = pl.ds(pl.multiple_of(k * SLICE, SLICE), SLICE)

                @pl.when(source != me)
                def _():
                    remote(src.at[0:RANK], dst.at[0, :, here], sd.at[0], recv.at[k], me, peer ^ 1).wait_recv()

                remote(src.at[0:RANK], dst.at[1, :, here], sd.at[0], recv.at[8 + k], me, peer ^ 1).wait_recv()
                grads = [dst[m, :, here].astype(F32) for m in range(2)]
                if gain:
                    grads = [grad * g_ref[:, cols] for grad in grads]
                mine = adam(*[state[2 * m + which, :, cols] for m in range(3)], grads[0])
                pair = adam(*[other[2 * m + which, :, here] for m in range(3)], grads[1])
                for m in range(3):
                    at = rows_each * which + RANK * m
                    half[at : at + RANK, here] = ((mine[m] + pair[m]) * 0.5).astype(BF16)
                return 0

            lax.fori_loop(0, 8, step, 0)

        def mean(*values):
            total = values[0].astype(F32)
            for value in values[1:]:
                total += value.astype(F32)
            return (total * (1.0 / len(values))).astype(BF16)

        def cols_at(at, width):
            return pl.ds(pl.multiple_of(at, 128), width)

        base = core * half_width
        pending = []
        count = iter(range(64))

        def send(src, dst, offset):
            k = next(count)
            copy = remote(src, dst, sj.at[k], rj.at[k], me, peer ^ offset)
            copy.start()
            return copy

        def out(rows):
            return outs[0] if rows.start == 0 else outs[1]

        def join(rows, at, width):
            there = out(rows).at[:, cols_at(base + at, width)]
            pending.append(send(there, there, 1))

        down, up = slice(0, rows_each), slice(rows_each, 2 * rows_each)

        def only_y(rows, at, width, land):
            copy = send(half.at[rows, at : at + width], land, 16)
            yield
            copy.wait()
            out(rows)[:, cols_at(base + at, width)] = mean(half[rows, at : at + width], land[...])
            join(rows, at, width)
            yield

        def z_first(rows, at, width, land_z, acc, land_y):
            part = width // group
            copies = [
                send(half.at[rows, cols_at(at + (rank ^ m) * part, part)], land_z.at[m - 1], offsets[m])
                for m in range(1, group)
            ]
            yield
            for copy in copies:
                copy.wait()
            acc[...] = mean(half[rows, cols_at(at + rank * part, part)], *[land_z[m] for m in range(group - 1)])
            copy = send(acc, land_y, 16)
            yield
            copy.wait()
            here = cols_at(base + at + rank * part, part)
            out(rows)[:, here] = mean(acc[...], land_y[...])
            copies = [send(out(rows).at[:, here], out(rows).at[:, here], offsets[m]) for m in range(1, group)]
            yield
            for copy in copies:
                copy.wait()
            join(rows, at, width)
            yield

        def y_first(rows, at, width, land_y, acc, land_z):
            wide = width // 2
            part = wide // group
            copy = send(half.at[rows, cols_at(at + (1 - far) * wide, wide)], land_y, 16)
            yield
            copy.wait()
            acc[...] = mean(half[rows, cols_at(at + far * wide, wide)], land_y[...])
            whole = cols_at(base + at + far * wide, wide)
            if group == 2:
                copies = [send(acc, land_z.at[0], offsets[1])]
            else:
                copies = [
                    send(acc.at[:, cols_at((rank ^ m) * part, part)], land_z.at[m - 1], offsets[m])
                    for m in range(1, group)
                ]
            yield
            for copy in copies:
                copy.wait()
            if group == 2:
                out(rows)[:, whole] = mean(acc[...], land_z[0])
            else:
                here = cols_at(base + at + far * wide + rank * part, part)
                own = acc[:, cols_at(rank * part, part)]
                out(rows)[:, here] = mean(own, *[land_z[m] for m in range(group - 1)])
                copies = [send(out(rows).at[:, here], out(rows).at[:, here], offsets[m]) for m in range(1, group)]
                yield
                for copy in copies:
                    copy.wait()
            copy = send(out(rows).at[:, whole], out(rows).at[:, whole], 16)
            yield
            copy.wait()
            join(rows, at, width)
            yield

        if not zbits:
            quarter = half_width // 2
            first = [only_y(down, 0, quarter, rest[0]), only_y(down, quarter, quarter, rest[1])]
            second = [only_y(up, 0, quarter, rest[2]), only_y(up, quarter, quarter, rest[3])]
        else:
            first = [z_first(down, 0, half_width, *rest[0:3])]
            second = []
            if turn < half_width:
                second.append(y_first(up, turn, half_width - turn, *rest[-3:]))
            if turn > 0:
                second.append(z_first(up, 0, turn, *rest[3:6]))

        adam_pairs(gdf, gd, rd, 0, True)
        if zbits:
            for chunk in first:
                next(chunk)
        adam_pairs(gup, gu, ru, 1, False)
        for chunk in second if zbits else first + second:
            next(chunk)
        chunks = first + second
        while chunks:
            chunks = [chunk for chunk in chunks if next(chunk, "end") != "end"]
        for copy in pending:
            copy.wait()
        scattered(gd, gdf, sd, rd)
        scattered(gu, gup, su, ru)

    dma = pltpu.SemaphoreType.DMA

    def blocks(*shape):
        return pltpu.VMEM(shape, BF16)

    scratch = CHAIN_SCRATCH + [
        blocks(6, RANK, WIDTH),
        blocks(6, RANK, half_width),
        blocks(6 * RANK, half_width),
        blocks(2, RANK, half_width),
        blocks(2, RANK, half_width),
    ]
    scratch += [dma((6,))] * 3 + [dma((SECTIONS,))] * 4 + [dma((32,))] * 2
    if not zbits:
        scratch += [blocks(rows_each, half_width // 2)] * 4
    else:
        for width in (half_width, turn) if turn else (half_width,):
            part = width // group
            scratch += [blocks(group - 1, rows_each, part), blocks(rows_each, part), blocks(rows_each, part)]
        if turn < half_width:
            wide = (half_width - turn) // 2
            part = wide if group == 2 else wide // group
            scratch += [blocks(rows_each, wide), blocks(rows_each, wide), blocks(group - 1, rows_each, part)]

    def update(*operands):
        return pl.pallas_call(
            kernel,
            out_shape=(jax.ShapeDtypeStruct((rows_each, WIDTH), BF16),) * 2,
            in_specs=[VMEM] * 10 + [pl.BlockSpec(memory_space=pl.ANY)] * 6,
            out_specs=(VMEM,) * 2,
            scratch_shapes=scratch,
            compiler_params=pltpu.CompilerParams(
                collective_id=1 + number, has_side_effects=True, vmem_limit_bytes=LIMIT
            ),
            name=f"update_{number}",
        )(*operands)

    return update


CASES = [(0, 4), (0, 1, 4), (0, 2, 4), (0, 1, 2, 4), (0, 3, 4), (0, 1, 3, 4), (0, 2, 3, 4)]


def on_device(hidden_in, cotangent, norm_gain, *rest):
    *state, round_bits = rest
    state = [
        jnp.swapaxes(array[0, 0], 0, 1) if number % 2 == 0 else array[0, 0] for number, array in enumerate(state)
    ]
    a, b = state[:2]
    h, q = hidden_in[0], cotangent[0]
    case, *chain = products(round_bits, h, q, norm_gain, a, b)
    branches = [make_update(bits, i) for i, bits in enumerate(CASES)]
    out = lax.switch(case[0], branches, *chain, h, q, norm_gain, *state)
    parts = [out[k % 2][RANK * (k // 2) : RANK * (k // 2) + RANK] for k in range(6)]
    return tuple((jnp.swapaxes(p, 0, 1) if k % 2 == 0 else p)[None, None] for k, p in enumerate(parts))


def solution(mesh):
    held = P("section", "peer", None, None)
    return jax.shard_map(
        on_device,
        mesh=mesh,
        in_specs=(P("peer", None, "section"), P("peer", None, "section"), P("section", None)) + (held,) * 6 + (P(),),
        out_specs=(held,) * 6,
        check_vma=False,
    )
```

```python
import jax
import jax.numpy as jnp
from jax import lax
from jax.experimental import pallas as pl
from jax.experimental.pallas import tpu as pltpu
from jax.sharding import PartitionSpec as P

ADAM_STEP = 100
MESH = pl.DeviceIdType.MESH
F32, BF16 = jnp.float32, jnp.bfloat16
SECTIONS, NX, NY = 16, 4, 4
RANK, WIDTH, TOKENS = 32, 4096, 128
SLICE = WIDTH // SECTIONS
ALL = SECTIONS * RANK
XW = ALL + 3 * TOKENS
SQ, WS, ZS = TOKENS, TOKENS + ALL, 2 * TOKENS + ALL
VMEM = pl.BlockSpec(memory_space=pltpu.VMEM)
SMEM = pl.BlockSpec(memory_space=pltpu.SMEM)
LIMIT = 48 << 20

NN = (((1,), (0,)), ((), ()))
NT = (((1,), (1,)), ((), ()))


def dot(a, b, dims=NN):
    return lax.dot_general(a, b, dims, preferred_element_type=F32)


def block_masks():
    row = lax.broadcasted_iota(jnp.int32, (ALL, ALL), 0) // RANK
    col = lax.broadcasted_iota(jnp.int32, (ALL, ALL), 1) // RANK
    return row > col, row < col


OFFSETS = [4 * dx + dy for dy in (2, 1, 3, 0) for dx in range(NX) if dx or dy]


def partner(me, j):
    return (me // NY + j // NY) % NX * NY + (me % NY + j % NY) % NY


def remote(src, dst, send, recv, section, peer):
    return pltpu.make_async_remote_copy(
        src_ref=src, dst_ref=dst, send_sem=send, recv_sem=recv, device_id=(section, peer), device_id_type=MESH
    )


CHUNKS = ((WS, 2 * TOKENS), (0, SQ + ALL // 2), (SQ + ALL // 2, ALL // 2))


def products_kernel(
    bits_hbm, h_hbm, q_hbm, g_hbm, a_hbm, b_hbm, case_ref, x_ref, af_ref, bf_ref, xt, lat, wp, rms,
    bits_ref, h_ref, q_ref, g_ref, a_ref, b_ref, loaded, n_ref, scaled, part, rx, px, ry, npart, nrx, npx, nry, sa, ra, sb, rb, sx, rxs, sy, rys, sg, rg, sh, rh, sn, rn, sm, rm,
):
    me, peer = lax.axis_index("section"), lax.axis_index("peer")
    mx, my = me // NY, me % NY

    operands = [(a_hbm, a_ref), (g_hbm, g_ref), (b_hbm, b_ref), (h_hbm, h_ref), (q_hbm, q_ref), (bits_hbm, bits_ref)]
    loads = [pltpu.make_async_copy(src, dst, loaded.at[k]) for k, (src, dst) in enumerate(operands)]
    for load in loads:
        load.start()
    barrier = pltpu.get_barrier_semaphore()
    for j in OFFSETS:
        pl.semaphore_signal(barrier, inc=1, device_id=(partner(me, j), peer), device_id_type=MESH)
    for load in loads:
        load.wait()
    case_ref[0] = sum(
        jnp.maximum(
            jnp.maximum((bits_ref[0] == bit).astype(jnp.int32), (bits_ref[1] == bit).astype(jnp.int32)),
            jnp.maximum((bits_ref[2] == bit).astype(jnp.int32), (bits_ref[3] == bit).astype(jnp.int32)),
        )
        << (bit - 1)
        for bit in (1, 2, 3)
    )
    scaled[...] = (a_ref[...].astype(F32) * (g_ref[...] * WIDTH**-0.5)).astype(BF16)
    pl.semaphore_wait(barrier, SECTIONS - 1)

    mine = pl.ds(pl.multiple_of(me * RANK, RANK), RANK)

    def scatter(src, dst, send, recv):
        copies = []
        for j in OFFSETS:
            to = partner(me, j)
            cols = pl.ds(pl.multiple_of(to * SLICE, SLICE), SLICE)
            copies.append(remote(src.at[:, cols], dst.at[mine], send.at[j], recv.at[j], to, peer))
        for copy in copies:
            copy.start()
        return copies

    b_copies = scatter(b_ref, bf_ref, sb, rb)
    a_copies = scatter(scaled, af_ref, sa, ra)
    cols = pl.ds(pl.multiple_of(me * SLICE, SLICE), SLICE)
    af_ref[mine, :] = scaled[:, cols]
    bf_ref[mine, :] = b_ref[:, cols]
    h = h_ref[...]
    square = h.astype(F32) * h.astype(F32)
    high = square.astype(BF16)
    low = (square - high.astype(F32)).astype(BF16)
    ones = jnp.ones((8, SLICE), BF16)
    npart[...] = dot(ones, high, NT) + dot(ones, low, NT)
    rs = RANK**-0.5

    def group_rows(x):
        return pl.ds(pl.multiple_of(x * NY * RANK, NY * RANK), NY * RANK)

    def rank_rows(y):
        return pl.ds(pl.multiple_of(y * RANK, RANK), RANK)

    held = [pl.ds(at, width) for at, width in CHUNKS]
    flying = [None] * len(CHUNKS)

    def started(copies):
        for copy in copies:
            copy.start()
        return copies

    def landed(c):
        for copy in flying[c]:
            copy.wait()

    def reduce_x(c):
        copies = []
        for j in range(1, NX):
            x, k = (mx + j) % NX, 4 * c + j
            to = x * NY + my
            copies.append(remote(part.at[group_rows(x), held[c]], rx.at[j - 1, :, held[c]], sx.at[k], rxs.at[k], to, peer))
            if c == 0:
                copies.append(remote(npart, nrx.at[j - 1], sn.at[j], rn.at[j], to, peer))
        flying[c] = started(copies)

    def reduce_y(c):
        landed(c)
        total = part[group_rows(mx), held[c]].astype(F32)
        for j in range(NX - 1):
            total += rx[j, :, held[c]].astype(F32)
        px[:, held[c]] = total.astype(BF16)
        if c == 0:
            npx[...] = npart[...] + nrx[0] + nrx[1] + nrx[2]
        copies = []
        for j in range(1, NY):
            y, k = (my + j) % NY, 4 * c + j
            to = mx * NY + y
            copies.append(remote(px.at[rank_rows(y), held[c]], ry.at[j - 1, :, held[c]], sy.at[k], rys.at[k], to, peer))
            if c == 0:
                copies.append(remote(npx, nry.at[j - 1], sm.at[j], rm.at[j], to, peer))
        flying[c] = started(copies)

    def gather_y(c):
        landed(c)
        total = px[rank_rows(my), held[c]].astype(F32)
        for j in range(NY - 1):
            total += ry[j, :, held[c]].astype(F32)
        x_ref[mine, held[c]] = total.astype(BF16)
        if c == 0:
            n_ref[...] = npx[...] + nry[0] + nry[1] + nry[2]
        rows = x_ref.at[mine, held[c]]
        flying[c] = started(
            [
                remote(rows, rows, sg.at[4 * c + j], rg.at[4 * c + j], mx * NY + (my + j) % NY, peer)
                for j in range(1, NY)
            ]
        )

    def gather_x(c):
        landed(c)
        rows = x_ref.at[group_rows(mx), held[c]]
        flying[c] = started(
            [
                remote(rows, rows, sh.at[4 * c + j], rh.at[4 * c + j], ((mx + j) % NX) * NY + my, peer)
                for j in range(1, NX)
            ]
        )

    for copy in b_copies:
        copy.wait()
    bf = bf_ref[...]
    part[:, WS:ZS] = (dot(bf, h, NT) * rs).astype(BF16)
    part[:, ZS:XW] = (dot(bf, q_ref[...], NT) * rs).astype(BF16)
    reduce_x(0)
    for copy in a_copies:
        copy.wait()
    af = af_ref[...]
    lower, _ = block_masks()

    def squares(at):
        other = bf_ref[at : at + ALL // 2, :]
        mask = lower[:, at : at + ALL // 2]
        products = jnp.where(mask, dot(af, other, NT) * rs, dot(bf, other, NT) * (1.0 / RANK))
        part[:, SQ + at : SQ + at + ALL // 2] = products.astype(BF16)

    part[:, 0:SQ] = dot(af, h, NT).astype(BF16)
    squares(0)
    reduce_x(1)
    squares(ALL // 2)
    reduce_x(2)
    reduce_y(0)
    reduce_y(1)
    gather_y(0)
    reduce_y(2)
    gather_y(1)
    gather_x(0)
    gather_y(2)
    gather_x(1)
    gather_x(2)
    landed(0)
    landed(1)
    norm = forward(range(SECTIONS // 2), n_ref[0:1, :], x_ref, xt, lat, wp, rms)
    landed(2)
    forward(range(SECTIONS // 2, SECTIONS), norm, x_ref, xt, lat, wp, rms)


def products(bits, h, q, gain, a, b):
    dma = pltpu.SemaphoreType.DMA
    group = NY * RANK
    return pl.pallas_call(
        products_kernel,
        out_shape=(
            jax.ShapeDtypeStruct((1,), jnp.int32),
            jax.ShapeDtypeStruct((ALL, XW), BF16),
            jax.ShapeDtypeStruct((ALL, SLICE), BF16),
            jax.ShapeDtypeStruct((ALL, SLICE), BF16),
            jax.ShapeDtypeStruct((ALL, ALL), BF16),
            jax.ShapeDtypeStruct((ALL, TOKENS), BF16),
            jax.ShapeDtypeStruct((ALL, TOKENS), F32),
            jax.ShapeDtypeStruct((SECTIONS, TOKENS), F32),
        ),
        in_specs=[pl.BlockSpec(memory_space=pl.ANY)] * 6,
        out_specs=(SMEM,) + (VMEM,) * 7,
        scratch_shapes=[
            pltpu.SMEM((4,), jnp.int32),
            pltpu.VMEM((TOKENS, SLICE), BF16),
            pltpu.VMEM((TOKENS, SLICE), BF16),
            pltpu.VMEM((1, WIDTH), F32),
            pltpu.VMEM((RANK, WIDTH), BF16),
            pltpu.VMEM((RANK, WIDTH), BF16),
            dma((6,)),
            pltpu.VMEM((8, TOKENS), F32),
            pltpu.VMEM((RANK, WIDTH), BF16),
            pltpu.VMEM((ALL, XW), BF16),
            pltpu.VMEM((NX - 1, group, XW), BF16),
            pltpu.VMEM((group, XW), BF16),
            pltpu.VMEM((NY - 1, RANK, XW), BF16),
            pltpu.VMEM((8, TOKENS), F32),
            pltpu.VMEM((NX - 1, 8, TOKENS), F32),
            pltpu.VMEM((8, TOKENS), F32),
            pltpu.VMEM((NY - 1, 8, TOKENS), F32),
        ]
        + [dma((SECTIONS,))] * 4
        + [dma((4 * len(CHUNKS),))] * 8
        + [dma((4,))] * 4,
        compiler_params=pltpu.CompilerParams(collective_id=0, has_side_effects=True, vmem_limit_bytes=LIMIT),
        name="products",
    )(bits, h, q, gain, a, b)


def rows_of(s):
    return slice(RANK * s, RANK * s + RANK)


def forward(sections, norm, x_ref, xt, lat, wp, rms):
    half = slice(RANK * sections[0], RANK * sections[-1] + RANK)
    xt[half, :] = x_ref[:, SQ + half.start : SQ + half.stop].astype(F32).T.astype(BF16)
    for s in sections:
        rows = rows_of(s)
        u = x_ref[rows, 0:SQ].astype(F32)
        w = x_ref[rows, WS:ZS].astype(F32)
        if s > 0:
            before = lat[0 : RANK * s, :]
            u += dot(x_ref[rows, SQ : SQ + RANK * s], before)
            w += dot(xt[rows, 0 : RANK * s], before)
        r = lax.rsqrt(jnp.maximum(norm, 0.0) * (1.0 / WIDTH) + 1e-5)
        latent = (u * r).astype(BF16)
        lat[rows, :] = latent
        after = w + dot(xt[rows, rows], latent)
        norm += jnp.sum(latent.astype(F32) * (w + after), axis=0, keepdims=True)
        wp[rows, :] = after
        rms[s : s + 1, :] = r
    return norm


def backward(x_ref, xt, lat, scaled_inner, cl, wp, rms):
    carry = jnp.zeros((1, TOKENS), F32)
    for s in reversed(range(SECTIONS)):
        rows = rows_of(s)
        inner = x_ref[rows, ZS:XW].astype(F32) - carry * wp[rows, :]
        if s < SECTIONS - 1:
            later = RANK * (s + 1)
            inner += dot(xt[rows, later:ALL], scaled_inner[later:ALL, :])
            inner -= dot(x_ref[rows, SQ + later : SQ + ALL], cl[later:ALL, :])
        r = rms[s : s + 1, :]
        latent = lat[rows, :].astype(F32)
        scaled_inner[rows, :] = (r * inner).astype(BF16)
        cl[rows, :] = (carry * latent).astype(BF16)
        carry += r * r * (jnp.sum(latent * inner, axis=0, keepdims=True) * (1.0 / WIDTH))


def down_gradient(af_ref, bf_ref, h_ref, lat, scaled_inner, gd_ref):
    lower, _ = block_masks()
    ri = scaled_inner[...]
    mixed = jnp.where(lower, dot(ri, lat[...], NT), 0.0).astype(BF16)
    down = dot(ri, h_ref[...]) + dot(mixed, bf_ref[...]) * RANK**-0.5
    gd_ref[...] = (down * WIDTH**-0.5).astype(BF16)


def up_gradient(af_ref, bf_ref, h_ref, q_ref, lat, scaled_inner, cl, gu_ref):
    _, upper = block_masks()
    rs = RANK**-0.5
    ls, ri, cls = lat[...], scaled_inner[...], cl[...]
    mixed = jnp.where(upper, dot(ls, cls, NT), dot(cls, ls, NT)).astype(BF16)
    up = dot(ls, q_ref[...]) - dot(cls, h_ref[...]) - dot(mixed, bf_ref[...]) * rs
    up += dot(jnp.where(upper, dot(ls, ri, NT), 0.0).astype(BF16), af_ref[...])
    gu_ref[...] = (up * rs).astype(BF16)


CHAIN_SCRATCH = [
    pltpu.VMEM((ALL, SLICE), BF16),
    pltpu.VMEM((ALL, SLICE), BF16),
    pltpu.VMEM((ALL, TOKENS), BF16),
    pltpu.VMEM((ALL, TOKENS), BF16),
]


def adam(param, first, second, grad):
    first_new = 0.9 * first.astype(F32) + 0.1 * grad
    second_new = 0.999 * second.astype(F32) + 0.001 * grad * grad
    corr_one = 1.0 - 0.9**ADAM_STEP
    corr_two = 1.0 - 0.999**ADAM_STEP
    update = 0.05 * (first_new / corr_one) / (jnp.sqrt(second_new / corr_two) + 1e-08)
    return param.astype(F32) - update, first_new, second_new


def make_update(bits, number):
    zbits = tuple(b for b in bits if b not in (0, 4))
    group = 1 << len(zbits)
    offsets = [sum(1 << b for i, b in enumerate(zbits) if m >> i & 1) for m in range(group)]
    half_width = WIDTH // 2
    rows_each = 3 * RANK
    turn = {(): half_width, (2,): 512, (3,): 512, (1, 2): half_width}.get(zbits, half_width // 2)

    def kernel(x_ref, af_ref, bf_ref, xt, lat, wp, rms, h_ref, q_ref, g_ref, *rest):
        held, outs, rest = rest[:6], rest[6:8], rest[8:]
        gd, gu, scaled_inner, cl = rest[:4]
        state, other, half, gdf, gup, sl, so, ro, sd, rd, su, ru, sj, rj = rest[4:18]
        rest = rest[18:]
        me, peer = lax.axis_index("section"), lax.axis_index("peer")
        core, far = peer % 2, peer // 16
        rank = sum(((peer // (1 << b)) % 2) * (1 << i) for i, b in enumerate(zbits)) if zbits else 0
        keeper = me // 8
        place = pl.ds(pl.multiple_of((me % 8) * SLICE, SLICE), SLICE)
        foreign = (core + keeper) % 2
        slot = foreign * 8 + me % 8

        loads = [pltpu.make_async_copy(held[k], state.at[k], sl.at[k]) for k in range(6)]
        for load in loads:
            load.start()
        barrier = pltpu.get_barrier_semaphore()

        def signal(section, to):
            pl.semaphore_signal(barrier, inc=1, device_id=(section, to), device_id_type=MESH)

        for k in range(8):
            source = core * 8 + k
            signal(source, peer + 1 - 2 * core)

            @pl.when(source != me)
            def _():
                signal(source, peer)

        partners = [1, 16] + offsets[1:]
        for offset in partners:
            signal(me, peer ^ offset)
        backward(x_ref, xt, lat, scaled_inner, cl, wp, rms)
        down_gradient(af_ref, bf_ref, h_ref, lat, scaled_inner, gd)
        pl.semaphore_wait(barrier, SECTIONS - 1 + foreign + len(partners))

        def gradient_copy(src, dst, send, recv, j):
            to = partner(me, j)
            rows = pl.ds(pl.multiple_of(to * RANK, RANK), RANK)
            return remote(
                src.at[rows], dst.at[foreign, :, place], send.at[j], recv.at[slot], to, peer - core + keeper
            )

        def scatter(src, dst, send, recv):
            for j in OFFSETS:
                gradient_copy(src, dst, send, recv, j).start()

            @pl.when(foreign == 1)
            def _():
                gradient_copy(src, dst, send, recv, 0).start()

            @pl.when(foreign == 0)
            def _():
                dst[0, :, place] = src[pl.ds(pl.multiple_of(me * RANK, RANK), RANK), :]

        def scattered(src, dst, send, recv):
            for j in OFFSETS:
                gradient_copy(src, dst, send, recv, j).wait_send()

            @pl.when(foreign == 1)
            def _():
                gradient_copy(src, dst, send, recv, 0).wait_send()

        scatter(gd, gdf, sd, rd)
        for load in loads:
            load.wait()
        theirs = pl.ds(pl.multiple_of((1 - core) * half_width, half_width), half_width)
        swaps = [remote(state.at[k, :, theirs], other.at[k], so.at[k], ro.at[k], me, peer ^ 1) for k in range(6)]
        for copy in swaps:
            copy.start()
        up_gradient(af_ref, bf_ref, h_ref, q_ref, lat, scaled_inner, cl, gu)
        scatter(gu, gup, su, ru)
        for copy in swaps:
            copy.wait()

        def adam_pairs(dst, src, recv, which, gain):
            def step(i, _):
                k = (me + i) % 8
                source = core * 8 + k
                cols = pl.ds(pl.multiple_of(source * SLICE, SLICE), SLICE)
                here = pl.ds(pl.multiple_of(k * SLICE, SLICE), SLICE)

                @pl.when(source != me)
                def _():
                    remote(src.at[0:RANK], dst.at[0, :, here], sd.at[0], recv.at[k], me, peer ^ 1).wait_recv()

                remote(src.at[0:RANK], dst.at[1, :, here], sd.at[0], recv.at[8 + k], me, peer ^ 1).wait_recv()
                grads = [dst[m, :, here].astype(F32) for m in range(2)]
                if gain:
                    grads = [grad * g_ref[:, cols] for grad in grads]
                mine = adam(*[state[2 * m + which, :, cols] for m in range(3)], grads[0])
                pair = adam(*[other[2 * m + which, :, here] for m in range(3)], grads[1])
                for m in range(3):
                    at = rows_each * which + RANK * m
                    half[at : at + RANK, here] = ((mine[m] + pair[m]) * 0.5).astype(BF16)
                return 0

            lax.fori_loop(0, 8, step, 0)

        def mean(*values):
            total = values[0].astype(F32)
            for value in values[1:]:
                total += value.astype(F32)
            return (total * (1.0 / len(values))).astype(BF16)

        def cols_at(at, width):
            return pl.ds(pl.multiple_of(at, 128), width)

        base = core * half_width
        pending = []
        count = iter(range(64))

        def send(src, dst, offset):
            k = next(count)
            copy = remote(src, dst, sj.at[k], rj.at[k], me, peer ^ offset)
            copy.start()
            return copy

        def out(rows):
            return outs[0] if rows.start == 0 else outs[1]

        def join(rows, at, width):
            there = out(rows).at[:, cols_at(base + at, width)]
            pending.append(send(there, there, 1))

        down, up = slice(0, rows_each), slice(rows_each, 2 * rows_each)

        def only_y(rows, at, width, land):
            copy = send(half.at[rows, at : at + width], land, 16)
            yield
            copy.wait()
            out(rows)[:, cols_at(base + at, width)] = mean(half[rows, at : at + width], land[...])
            join(rows, at, width)
            yield

        def z_first(rows, at, width, land_z, acc, land_y):
            part = width // group
            copies = [
                send(half.at[rows, cols_at(at + (rank ^ m) * part, part)], land_z.at[m - 1], offsets[m])
                for m in range(1, group)
            ]
            yield
            for copy in copies:
                copy.wait()
            acc[...] = mean(half[rows, cols_at(at + rank * part, part)], *[land_z[m] for m in range(group - 1)])
            copy = send(acc, land_y, 16)
            yield
            copy.wait()
            here = cols_at(base + at + rank * part, part)
            out(rows)[:, here] = mean(acc[...], land_y[...])
            copies = [send(out(rows).at[:, here], out(rows).at[:, here], offsets[m]) for m in range(1, group)]
            yield
            for copy in copies:
                copy.wait()
            join(rows, at, width)
            yield

        def y_first(rows, at, width, land_y, acc, land_z):
            wide = width // 2
            part = wide // group
            copy = send(half.at[rows, cols_at(at + (1 - far) * wide, wide)], land_y, 16)
            yield
            copy.wait()
            acc[...] = mean(half[rows, cols_at(at + far * wide, wide)], land_y[...])
            whole = cols_at(base + at + far * wide, wide)
            if group == 2:
                copies = [send(acc, land_z.at[0], offsets[1])]
            else:
                copies = [
                    send(acc.at[:, cols_at((rank ^ m) * part, part)], land_z.at[m - 1], offsets[m])
                    for m in range(1, group)
                ]
            yield
            for copy in copies:
                copy.wait()
            if group == 2:
                out(rows)[:, whole] = mean(acc[...], land_z[0])
            else:
                here = cols_at(base + at + far * wide + rank * part, part)
                own = acc[:, cols_at(rank * part, part)]
                out(rows)[:, here] = mean(own, *[land_z[m] for m in range(group - 1)])
                copies = [send(out(rows).at[:, here], out(rows).at[:, here], offsets[m]) for m in range(1, group)]
                yield
                for copy in copies:
                    copy.wait()
            copy = send(out(rows).at[:, whole], out(rows).at[:, whole], 16)
            yield
            copy.wait()
            join(rows, at, width)
            yield

        if not zbits:
            quarter = half_width // 2
            first = [only_y(down, 0, quarter, rest[0]), only_y(down, quarter, quarter, rest[1])]
            second = [only_y(up, 0, quarter, rest[2]), only_y(up, quarter, quarter, rest[3])]
        else:
            first = [z_first(down, 0, half_width, *rest[0:3])]
            second = []
            if turn < half_width:
                second.append(y_first(up, turn, half_width - turn, *rest[-3:]))
            if turn > 0:
                second.append(z_first(up, 0, turn, *rest[3:6]))

        adam_pairs(gdf, gd, rd, 0, True)
        if zbits:
            for chunk in first:
                next(chunk)
        adam_pairs(gup, gu, ru, 1, False)
        for chunk in second if zbits else first + second:
            next(chunk)
        chunks = second + first if group > 2 and turn < half_width else first + second[::-1]
        while chunks:
            chunks = [chunk for chunk in chunks if next(chunk, "end") != "end"]
        for copy in pending:
            copy.wait()
        scattered(gd, gdf, sd, rd)
        scattered(gu, gup, su, ru)

    dma = pltpu.SemaphoreType.DMA

    def blocks(*shape):
        return pltpu.VMEM(shape, BF16)

    scratch = CHAIN_SCRATCH + [
        blocks(6, RANK, WIDTH),
        blocks(6, RANK, half_width),
        blocks(6 * RANK, half_width),
        blocks(2, RANK, half_width),
        blocks(2, RANK, half_width),
    ]
    scratch += [dma((6,))] * 3 + [dma((SECTIONS,))] * 4 + [dma((32,))] * 2
    if not zbits:
        scratch += [blocks(rows_each, half_width // 2)] * 4
    else:
        for width in (half_width, turn) if turn else (half_width,):
            part = width // group
            scratch += [blocks(group - 1, rows_each, part), blocks(rows_each, part), blocks(rows_each, part)]
        if turn < half_width:
            wide = (half_width - turn) // 2
            part = wide if group == 2 else wide // group
            scratch += [blocks(rows_each, wide), blocks(rows_each, wide), blocks(group - 1, rows_each, part)]

    def update(*operands):
        return pl.pallas_call(
            kernel,
            out_shape=(jax.ShapeDtypeStruct((rows_each, WIDTH), BF16),) * 2,
            in_specs=[VMEM] * 10 + [pl.BlockSpec(memory_space=pl.ANY)] * 6,
            out_specs=(VMEM,) * 2,
            scratch_shapes=scratch,
            compiler_params=pltpu.CompilerParams(
                collective_id=1 + number, has_side_effects=True, vmem_limit_bytes=LIMIT
            ),
            name=f"update_{number}",
        )(*operands)

    return update


CASES = [(0, 4), (0, 1, 4), (0, 2, 4), (0, 1, 2, 4), (0, 3, 4), (0, 1, 3, 4), (0, 2, 3, 4)]


def on_device(hidden_in, cotangent, norm_gain, *rest):
    *state, round_bits = rest
    state = [
        jnp.swapaxes(array[0, 0], 0, 1) if number % 2 == 0 else array[0, 0] for number, array in enumerate(state)
    ]
    a, b = state[:2]
    h, q = hidden_in[0], cotangent[0]
    case, *chain = products(round_bits, h, q, norm_gain, a, b)
    branches = [make_update(bits, i) for i, bits in enumerate(CASES)]
    out = lax.switch(case[0], branches, *chain, h, q, norm_gain, *state)
    parts = [out[k % 2][RANK * (k // 2) : RANK * (k // 2) + RANK] for k in range(6)]
    return tuple((jnp.swapaxes(p, 0, 1) if k % 2 == 0 else p)[None, None] for k, p in enumerate(parts))


def solution(mesh):
    held = P("section", "peer", None, None)
    return jax.shard_map(
        on_device,
        mesh=mesh,
        in_specs=(P("peer", None, "section"), P("peer", None, "section"), P("section", None)) + (held,) * 6 + (P(),),
        out_specs=(held,) * 6,
        check_vma=False,
    )
```

```python
import jax
import jax.numpy as jnp
from jax import lax
from jax.experimental import pallas as pl
from jax.experimental.pallas import tpu as pltpu
from jax.sharding import PartitionSpec as P

ADAM_STEP = 100
MESH = pl.DeviceIdType.MESH
F32, BF16 = jnp.float32, jnp.bfloat16
SECTIONS, NX, NY = 16, 4, 4
RANK, WIDTH, TOKENS = 32, 4096, 128
SLICE = WIDTH // SECTIONS
ALL = SECTIONS * RANK
XW = ALL + 3 * TOKENS
SQ, WS, ZS = TOKENS, TOKENS + ALL, 2 * TOKENS + ALL
VMEM = pl.BlockSpec(memory_space=pltpu.VMEM)
SMEM = pl.BlockSpec(memory_space=pltpu.SMEM)
LIMIT = 48 << 20

NN = (((1,), (0,)), ((), ()))
NT = (((1,), (1,)), ((), ()))


def dot(a, b, dims=NN):
    return lax.dot_general(a, b, dims, preferred_element_type=F32)


def block_masks():
    row = lax.broadcasted_iota(jnp.int32, (ALL, ALL), 0) // RANK
    col = lax.broadcasted_iota(jnp.int32, (ALL, ALL), 1) // RANK
    return row > col, row < col


OFFSETS = [4 * dx + dy for dy in (2, 1, 3, 0) for dx in range(NX) if dx or dy]


def partner(me, j):
    return (me // NY + j // NY) % NX * NY + (me % NY + j % NY) % NY


def remote(src, dst, send, recv, section, peer):
    return pltpu.make_async_remote_copy(
        src_ref=src, dst_ref=dst, send_sem=send, recv_sem=recv, device_id=(section, peer), device_id_type=MESH
    )


CHUNKS = ((WS, 2 * TOKENS), (0, SQ + ALL // 2), (SQ + ALL // 2, ALL // 2))


def products_kernel(
    bits_hbm, h_hbm, q_hbm, g_hbm, a_hbm, b_hbm, case_ref, x_ref, af_ref, bf_ref, xt, lat, wp, rms,
    bits_ref, h_ref, q_ref, g_ref, a_ref, b_ref, loaded, n_ref, scaled, part, rx, px, ry, npart, nrx, npx, nry, sa, ra, sb, rb, sx, rxs, sy, rys, sg, rg, sh, rh, sn, rn, sm, rm,
):
    me, peer = lax.axis_index("section"), lax.axis_index("peer")
    mx, my = me // NY, me % NY

    operands = [(a_hbm, a_ref), (g_hbm, g_ref), (b_hbm, b_ref), (h_hbm, h_ref), (q_hbm, q_ref), (bits_hbm, bits_ref)]
    loads = [pltpu.make_async_copy(src, dst, loaded.at[k]) for k, (src, dst) in enumerate(operands)]
    for load in loads:
        load.start()
    barrier = pltpu.get_barrier_semaphore()
    for j in OFFSETS:
        pl.semaphore_signal(barrier, inc=1, device_id=(partner(me, j), peer), device_id_type=MESH)
    for load in loads:
        load.wait()
    case_ref[0] = sum(
        jnp.maximum(
            jnp.maximum((bits_ref[0] == bit).astype(jnp.int32), (bits_ref[1] == bit).astype(jnp.int32)),
            jnp.maximum((bits_ref[2] == bit).astype(jnp.int32), (bits_ref[3] == bit).astype(jnp.int32)),
        )
        << (bit - 1)
        for bit in (1, 2, 3)
    )
    scaled[...] = (a_ref[...].astype(F32) * (g_ref[...] * WIDTH**-0.5)).astype(BF16)
    pl.semaphore_wait(barrier, SECTIONS - 1)

    mine = pl.ds(pl.multiple_of(me * RANK, RANK), RANK)

    def scatter(src, dst, send, recv):
        copies = []
        for j in OFFSETS:
            to = partner(me, j)
            cols = pl.ds(pl.multiple_of(to * SLICE, SLICE), SLICE)
            copies.append(remote(src.at[:, cols], dst.at[mine], send.at[j], recv.at[j], to, peer))
        for copy in copies:
            copy.start()
        return copies

    b_copies = scatter(b_ref, bf_ref, sb, rb)
    a_copies = scatter(scaled, af_ref, sa, ra)
    cols = pl.ds(pl.multiple_of(me * SLICE, SLICE), SLICE)
    af_ref[mine, :] = scaled[:, cols]
    bf_ref[mine, :] = b_ref[:, cols]
    h = h_ref[...]
    square = h.astype(F32) * h.astype(F32)
    high = square.astype(BF16)
    low = (square - high.astype(F32)).astype(BF16)
    ones = jnp.ones((8, SLICE), BF16)
    npart[...] = dot(ones, high, NT) + dot(ones, low, NT)
    rs = RANK**-0.5

    def group_rows(x):
        return pl.ds(pl.multiple_of(x * NY * RANK, NY * RANK), NY * RANK)

    def rank_rows(y):
        return pl.ds(pl.multiple_of(y * RANK, RANK), RANK)

    held = [pl.ds(at, width) for at, width in CHUNKS]
    flying = [None] * len(CHUNKS)

    def started(copies):
        for copy in copies:
            copy.start()
        return copies

    def landed(c):
        for copy in flying[c]:
            copy.wait()

    def reduce_x(c):
        copies = []
        for j in range(1, NX):
            x, k = (mx + j) % NX, 4 * c + j
            to = x * NY + my
            copies.append(remote(part.at[group_rows(x), held[c]], rx.at[j - 1, :, held[c]], sx.at[k], rxs.at[k], to, peer))
            if c == 0:
                copies.append(remote(npart, nrx.at[j - 1], sn.at[j], rn.at[j], to, peer))
        flying[c] = started(copies)

    def reduce_y(c):
        landed(c)
        total = part[group_rows(mx), held[c]].astype(F32)
        for j in range(NX - 1):
            total += rx[j, :, held[c]].astype(F32)
        px[:, held[c]] = total.astype(BF16)
        if c == 0:
            npx[...] = npart[...] + nrx[0] + nrx[1] + nrx[2]
        copies = []
        for j in range(1, NY):
            y, k = (my + j) % NY, 4 * c + j
            to = mx * NY + y
            copies.append(remote(px.at[rank_rows(y), held[c]], ry.at[j - 1, :, held[c]], sy.at[k], rys.at[k], to, peer))
            if c == 0:
                copies.append(remote(npx, nry.at[j - 1], sm.at[j], rm.at[j], to, peer))
        flying[c] = started(copies)

    def gather_y(c):
        landed(c)
        total = px[rank_rows(my), held[c]].astype(F32)
        for j in range(NY - 1):
            total += ry[j, :, held[c]].astype(F32)
        x_ref[mine, held[c]] = total.astype(BF16)
        if c == 0:
            n_ref[...] = npx[...] + nry[0] + nry[1] + nry[2]
        rows = x_ref.at[mine, held[c]]
        flying[c] = started(
            [
                remote(rows, rows, sg.at[4 * c + j], rg.at[4 * c + j], mx * NY + (my + j) % NY, peer)
                for j in range(1, NY)
            ]
        )

    def gather_x(c):
        landed(c)
        rows = x_ref.at[group_rows(mx), held[c]]
        flying[c] = started(
            [
                remote(rows, rows, sh.at[4 * c + j], rh.at[4 * c + j], ((mx + j) % NX) * NY + my, peer)
                for j in range(1, NX)
            ]
        )

    for copy in b_copies:
        copy.wait()
    bf = bf_ref[...]
    part[:, WS:ZS] = (dot(bf, h, NT) * rs).astype(BF16)
    part[:, ZS:XW] = (dot(bf, q_ref[...], NT) * rs).astype(BF16)
    reduce_x(0)
    for copy in a_copies:
        copy.wait()
    af = af_ref[...]
    lower, _ = block_masks()

    def squares(at):
        other = bf_ref[at : at + ALL // 2, :]
        mask = lower[:, at : at + ALL // 2]
        products = jnp.where(mask, dot(af, other, NT) * rs, dot(bf, other, NT) * (1.0 / RANK))
        part[:, SQ + at : SQ + at + ALL // 2] = products.astype(BF16)

    part[:, 0:SQ] = dot(af, h, NT).astype(BF16)
    squares(0)
    reduce_x(1)
    squares(ALL // 2)
    reduce_x(2)
    reduce_y(0)
    reduce_y(1)
    gather_y(0)
    reduce_y(2)
    gather_y(1)
    gather_x(0)
    gather_y(2)
    gather_x(1)
    gather_x(2)
    landed(0)
    landed(1)
    norm = forward(range(SECTIONS // 2), n_ref[0:1, :], x_ref, xt, lat, wp, rms)
    landed(2)
    forward(range(SECTIONS // 2, SECTIONS), norm, x_ref, xt, lat, wp, rms)


def products(bits, h, q, gain, a, b):
    dma = pltpu.SemaphoreType.DMA
    group = NY * RANK
    return pl.pallas_call(
        products_kernel,
        out_shape=(
            jax.ShapeDtypeStruct((1,), jnp.int32),
            jax.ShapeDtypeStruct((ALL, XW), BF16),
            jax.ShapeDtypeStruct((ALL, SLICE), BF16),
            jax.ShapeDtypeStruct((ALL, SLICE), BF16),
            jax.ShapeDtypeStruct((ALL, ALL), BF16),
            jax.ShapeDtypeStruct((ALL, TOKENS), BF16),
            jax.ShapeDtypeStruct((ALL, TOKENS), F32),
            jax.ShapeDtypeStruct((SECTIONS, TOKENS), F32),
        ),
        in_specs=[pl.BlockSpec(memory_space=pl.ANY)] * 6,
        out_specs=(SMEM,) + (VMEM,) * 7,
        scratch_shapes=[
            pltpu.SMEM((4,), jnp.int32),
            pltpu.VMEM((TOKENS, SLICE), BF16),
            pltpu.VMEM((TOKENS, SLICE), BF16),
            pltpu.VMEM((1, WIDTH), F32),
            pltpu.VMEM((RANK, WIDTH), BF16),
            pltpu.VMEM((RANK, WIDTH), BF16),
            dma((6,)),
            pltpu.VMEM((8, TOKENS), F32),
            pltpu.VMEM((RANK, WIDTH), BF16),
            pltpu.VMEM((ALL, XW), BF16),
            pltpu.VMEM((NX - 1, group, XW), BF16),
            pltpu.VMEM((group, XW), BF16),
            pltpu.VMEM((NY - 1, RANK, XW), BF16),
            pltpu.VMEM((8, TOKENS), F32),
            pltpu.VMEM((NX - 1, 8, TOKENS), F32),
            pltpu.VMEM((8, TOKENS), F32),
            pltpu.VMEM((NY - 1, 8, TOKENS), F32),
        ]
        + [dma((SECTIONS,))] * 4
        + [dma((4 * len(CHUNKS),))] * 8
        + [dma((4,))] * 4,
        compiler_params=pltpu.CompilerParams(collective_id=0, has_side_effects=True, vmem_limit_bytes=LIMIT),
        name="products",
    )(bits, h, q, gain, a, b)


def rows_of(s):
    return slice(RANK * s, RANK * s + RANK)


def forward(sections, norm, x_ref, xt, lat, wp, rms):
    half = slice(RANK * sections[0], RANK * sections[-1] + RANK)
    xt[half, :] = x_ref[:, SQ + half.start : SQ + half.stop].astype(F32).T.astype(BF16)
    for s in sections:
        rows = rows_of(s)
        u = x_ref[rows, 0:SQ].astype(F32)
        w = x_ref[rows, WS:ZS].astype(F32)
        if s > 0:
            before = lat[0 : RANK * s, :]
            u += dot(x_ref[rows, SQ : SQ + RANK * s], before)
            w += dot(xt[rows, 0 : RANK * s], before)
        r = lax.rsqrt(jnp.maximum(norm, 0.0) * (1.0 / WIDTH) + 1e-5)
        latent = (u * r).astype(BF16)
        lat[rows, :] = latent
        after = w + dot(xt[rows, rows], latent)
        norm += jnp.sum(latent.astype(F32) * (w + after), axis=0, keepdims=True)
        wp[rows, :] = after
        rms[s : s + 1, :] = r
    return norm


def backward(x_ref, xt, lat, scaled_inner, cl, wp, rms):
    carry = jnp.zeros((1, TOKENS), F32)
    for s in reversed(range(SECTIONS)):
        rows = rows_of(s)
        inner = x_ref[rows, ZS:XW].astype(F32) - carry * wp[rows, :]
        if s < SECTIONS - 1:
            later = RANK * (s + 1)
            inner += dot(xt[rows, later:ALL], scaled_inner[later:ALL, :])
            inner -= dot(x_ref[rows, SQ + later : SQ + ALL], cl[later:ALL, :])
        r = rms[s : s + 1, :]
        latent = lat[rows, :].astype(F32)
        scaled_inner[rows, :] = (r * inner).astype(BF16)
        cl[rows, :] = (carry * latent).astype(BF16)
        carry += r * r * (jnp.sum(latent * inner, axis=0, keepdims=True) * (1.0 / WIDTH))


def down_gradient(af_ref, bf_ref, h_ref, lat, scaled_inner, gd_ref):
    lower, _ = block_masks()
    ri = scaled_inner[...]
    mixed = jnp.where(lower, dot(ri, lat[...], NT), 0.0).astype(BF16)
    down = dot(ri, h_ref[...]) + dot(mixed, bf_ref[...]) * RANK**-0.5
    gd_ref[...] = (down * WIDTH**-0.5).astype(BF16)


def up_gradient(af_ref, bf_ref, h_ref, q_ref, lat, scaled_inner, cl, gu_ref):
    _, upper = block_masks()
    rs = RANK**-0.5
    ls, ri, cls = lat[...], scaled_inner[...], cl[...]
    mixed = jnp.where(upper, dot(ls, cls, NT), dot(cls, ls, NT)).astype(BF16)
    up = dot(ls, q_ref[...]) - dot(cls, h_ref[...]) - dot(mixed, bf_ref[...]) * rs
    up += dot(jnp.where(upper, dot(ls, ri, NT), 0.0).astype(BF16), af_ref[...])
    gu_ref[...] = (up * rs).astype(BF16)


CHAIN_SCRATCH = [
    pltpu.VMEM((ALL, SLICE), BF16),
    pltpu.VMEM((ALL, SLICE), BF16),
    pltpu.VMEM((ALL, TOKENS), BF16),
    pltpu.VMEM((ALL, TOKENS), BF16),
]


def adam(param, first, second, grad):
    first_new = 0.9 * first.astype(F32) + 0.1 * grad
    second_new = 0.999 * second.astype(F32) + 0.001 * grad * grad
    corr_one = 1.0 - 0.9**ADAM_STEP
    corr_two = 1.0 - 0.999**ADAM_STEP
    update = 0.05 * (first_new / corr_one) / (jnp.sqrt(second_new / corr_two) + 1e-08)
    return param.astype(F32) - update, first_new, second_new


def make_update(bits, number):
    zbits = tuple(b for b in bits if b not in (0, 4))
    group = 1 << len(zbits)
    offsets = [sum(1 << b for i, b in enumerate(zbits) if m >> i & 1) for m in range(group)]
    half_width = WIDTH // 2
    rows_each = 3 * RANK
    turn = {(): half_width, (2,): 512, (3,): 512}.get(zbits, half_width // 2)

    def kernel(x_ref, af_ref, bf_ref, xt, lat, wp, rms, h_ref, q_ref, g_ref, *rest):
        held, outs, rest = rest[:6], rest[6:8], rest[8:]
        gd, gu, scaled_inner, cl = rest[:4]
        state, other, half, gdf, gup, sl, so, ro, sd, rd, su, ru, sj, rj = rest[4:18]
        rest = rest[18:]
        me, peer = lax.axis_index("section"), lax.axis_index("peer")
        core, far = peer % 2, peer // 16
        rank = sum(((peer // (1 << b)) % 2) * (1 << i) for i, b in enumerate(zbits)) if zbits else 0
        keeper = me // 8
        place = pl.ds(pl.multiple_of((me % 8) * SLICE, SLICE), SLICE)
        foreign = (core + keeper) % 2
        slot = foreign * 8 + me % 8

        loads = [pltpu.make_async_copy(held[k], state.at[k], sl.at[k]) for k in range(6)]
        for load in loads:
            load.start()
        barrier = pltpu.get_barrier_semaphore()

        def signal(section, to):
            pl.semaphore_signal(barrier, inc=1, device_id=(section, to), device_id_type=MESH)

        for k in range(8):
            source = core * 8 + k
            signal(source, peer + 1 - 2 * core)

            @pl.when(source != me)
            def _():
                signal(source, peer)

        partners = [1, 16] + offsets[1:]
        for offset in partners:
            signal(me, peer ^ offset)
        backward(x_ref, xt, lat, scaled_inner, cl, wp, rms)
        down_gradient(af_ref, bf_ref, h_ref, lat, scaled_inner, gd)
        pl.semaphore_wait(barrier, SECTIONS - 1 + foreign + len(partners))

        def gradient_copy(src, dst, send, recv, j):
            to = partner(me, j)
            rows = pl.ds(pl.multiple_of(to * RANK, RANK), RANK)
            return remote(
                src.at[rows], dst.at[foreign, :, place], send.at[j], recv.at[slot], to, peer - core + keeper
            )

        def scatter(src, dst, send, recv):
            for j in OFFSETS:
                gradient_copy(src, dst, send, recv, j).start()

            @pl.when(foreign == 1)
            def _():
                gradient_copy(src, dst, send, recv, 0).start()

            @pl.when(foreign == 0)
            def _():
                dst[0, :, place] = src[pl.ds(pl.multiple_of(me * RANK, RANK), RANK), :]

        def scattered(src, dst, send, recv):
            for j in OFFSETS:
                gradient_copy(src, dst, send, recv, j).wait_send()

            @pl.when(foreign == 1)
            def _():
                gradient_copy(src, dst, send, recv, 0).wait_send()

        scatter(gd, gdf, sd, rd)
        for load in loads:
            load.wait()
        theirs = pl.ds(pl.multiple_of((1 - core) * half_width, half_width), half_width)
        swaps = [remote(state.at[k, :, theirs], other.at[k], so.at[k], ro.at[k], me, peer ^ 1) for k in range(6)]
        for copy in swaps:
            copy.start()
        up_gradient(af_ref, bf_ref, h_ref, q_ref, lat, scaled_inner, cl, gu)
        scatter(gu, gup, su, ru)
        for copy in swaps:
            copy.wait()

        def adam_pairs(dst, src, recv, which, gain):
            def step(i, _):
                k = (me + i) % 8
                source = core * 8 + k
                cols = pl.ds(pl.multiple_of(source * SLICE, SLICE), SLICE)
                here = pl.ds(pl.multiple_of(k * SLICE, SLICE), SLICE)

                @pl.when(source != me)
                def _():
                    remote(src.at[0:RANK], dst.at[0, :, here], sd.at[0], recv.at[k], me, peer ^ 1).wait_recv()

                remote(src.at[0:RANK], dst.at[1, :, here], sd.at[0], recv.at[8 + k], me, peer ^ 1).wait_recv()
                grads = [dst[m, :, here].astype(F32) for m in range(2)]
                if gain:
                    grads = [grad * g_ref[:, cols] for grad in grads]
                mine = adam(*[state[2 * m + which, :, cols] for m in range(3)], grads[0])
                pair = adam(*[other[2 * m + which, :, here] for m in range(3)], grads[1])
                for m in range(3):
                    at = rows_each * which + RANK * m
                    half[at : at + RANK, here] = ((mine[m] + pair[m]) * 0.5).astype(BF16)
                return 0

            lax.fori_loop(0, 8, step, 0)

        def mean(*values):
            total = values[0].astype(F32)
            for value in values[1:]:
                total += value.astype(F32)
            return (total * (1.0 / len(values))).astype(BF16)

        def cols_at(at, width):
            return pl.ds(pl.multiple_of(at, 128), width)

        base = core * half_width
        pending = []
        count = iter(range(64))

        def send(src, dst, offset):
            k = next(count)
            copy = remote(src, dst, sj.at[k], rj.at[k], me, peer ^ offset)
            copy.start()
            return copy

        def out(rows):
            return outs[0] if rows.start == 0 else outs[1]

        def join(rows, at, width):
            there = out(rows).at[:, cols_at(base + at, width)]
            pending.append(send(there, there, 1))

        down, up = slice(0, rows_each), slice(rows_each, 2 * rows_each)

        def only_y(rows, at, width, land):
            copy = send(half.at[rows, at : at + width], land, 16)
            yield
            copy.wait()
            out(rows)[:, cols_at(base + at, width)] = mean(half[rows, at : at + width], land[...])
            join(rows, at, width)
            yield

        def z_first(rows, at, width, land_z, acc, land_y):
            part = width // group
            copies = [
                send(half.at[rows, cols_at(at + (rank ^ m) * part, part)], land_z.at[m - 1], offsets[m])
                for m in range(1, group)
            ]
            yield
            for copy in copies:
                copy.wait()
            acc[...] = mean(half[rows, cols_at(at + rank * part, part)], *[land_z[m] for m in range(group - 1)])
            copy = send(acc, land_y, 16)
            yield
            copy.wait()
            here = cols_at(base + at + rank * part, part)
            out(rows)[:, here] = mean(acc[...], land_y[...])
            copies = [send(out(rows).at[:, here], out(rows).at[:, here], offsets[m]) for m in range(1, group)]
            yield
            for copy in copies:
                copy.wait()
            join(rows, at, width)
            yield

        def y_first(rows, at, width, land_y, acc, land_z):
            wide = width // 2
            part = wide // group
            copy = send(half.at[rows, cols_at(at + (1 - far) * wide, wide)], land_y, 16)
            yield
            copy.wait()
            acc[...] = mean(half[rows, cols_at(at + far * wide, wide)], land_y[...])
            whole = cols_at(base + at + far * wide, wide)
            if group == 2:
                copies = [send(acc, land_z.at[0], offsets[1])]
            else:
                copies = [
                    send(acc.at[:, cols_at((rank ^ m) * part, part)], land_z.at[m - 1], offsets[m])
                    for m in range(1, group)
                ]
            yield
            for copy in copies:
                copy.wait()
            if group == 2:
                out(rows)[:, whole] = mean(acc[...], land_z[0])
            else:
                here = cols_at(base + at + far * wide + rank * part, part)
                own = acc[:, cols_at(rank * part, part)]
                out(rows)[:, here] = mean(own, *[land_z[m] for m in range(group - 1)])
                copies = [send(out(rows).at[:, here], out(rows).at[:, here], offsets[m]) for m in range(1, group)]
                yield
                for copy in copies:
                    copy.wait()
            copy = send(out(rows).at[:, whole], out(rows).at[:, whole], 16)
            yield
            copy.wait()
            join(rows, at, width)
            yield

        if not zbits:
            quarter = half_width // 2
            first = [only_y(down, 0, quarter, rest[0]), only_y(down, quarter, quarter, rest[1])]
            second = [only_y(up, 0, quarter, rest[2]), only_y(up, quarter, quarter, rest[3])]
        else:
            first = [z_first(down, 0, half_width, *rest[0:3])]
            second = []
            if turn < half_width:
                second.append(y_first(up, turn, half_width - turn, *rest[-3:]))
            if turn > 0:
                second.append(z_first(up, 0, turn, *rest[3:6]))

        adam_pairs(gdf, gd, rd, 0, True)
        if zbits:
            for chunk in first:
                next(chunk)
        adam_pairs(gup, gu, ru, 1, False)
        for chunk in second if zbits else first + second:
            next(chunk)
        chunks = second + first if group > 2 and turn < half_width else first + second[::-1]
        while chunks:
            chunks = [chunk for chunk in chunks if next(chunk, "end") != "end"]
        for copy in pending:
            copy.wait()
        scattered(gd, gdf, sd, rd)
        scattered(gu, gup, su, ru)

    dma = pltpu.SemaphoreType.DMA

    def blocks(*shape):
        return pltpu.VMEM(shape, BF16)

    scratch = CHAIN_SCRATCH + [
        blocks(6, RANK, WIDTH),
        blocks(6, RANK, half_width),
        blocks(6 * RANK, half_width),
        blocks(2, RANK, half_width),
        blocks(2, RANK, half_width),
    ]
    scratch += [dma((6,))] * 3 + [dma((SECTIONS,))] * 4 + [dma((32,))] * 2
    if not zbits:
        scratch += [blocks(rows_each, half_width // 2)] * 4
    else:
        for width in (half_width, turn) if turn else (half_width,):
            part = width // group
            scratch += [blocks(group - 1, rows_each, part), blocks(rows_each, part), blocks(rows_each, part)]
        if turn < half_width:
            wide = (half_width - turn) // 2
            part = wide if group == 2 else wide // group
            scratch += [blocks(rows_each, wide), blocks(rows_each, wide), blocks(group - 1, rows_each, part)]

    def update(*operands):
        return pl.pallas_call(
            kernel,
            out_shape=(jax.ShapeDtypeStruct((rows_each, WIDTH), BF16),) * 2,
            in_specs=[VMEM] * 10 + [pl.BlockSpec(memory_space=pl.ANY)] * 6,
            out_specs=(VMEM,) * 2,
            scratch_shapes=scratch,
            compiler_params=pltpu.CompilerParams(
                collective_id=1 + number, has_side_effects=True, vmem_limit_bytes=LIMIT
            ),
            name=f"update_{number}",
        )(*operands)

    return update


CASES = [(0, 4), (0, 1, 4), (0, 2, 4), (0, 1, 2, 4), (0, 3, 4), (0, 1, 3, 4), (0, 2, 3, 4)]


def on_device(hidden_in, cotangent, norm_gain, *rest):
    *state, round_bits = rest
    state = [
        jnp.swapaxes(array[0, 0], 0, 1) if number % 2 == 0 else array[0, 0] for number, array in enumerate(state)
    ]
    a, b = state[:2]
    h, q = hidden_in[0], cotangent[0]
    case, *chain = products(round_bits, h, q, norm_gain, a, b)
    branches = [make_update(bits, i) for i, bits in enumerate(CASES)]
    out = lax.switch(case[0], branches, *chain, h, q, norm_gain, *state)
    parts = [out[k % 2][RANK * (k // 2) : RANK * (k // 2) + RANK] for k in range(6)]
    return tuple((jnp.swapaxes(p, 0, 1) if k % 2 == 0 else p)[None, None] for k, p in enumerate(parts))


def solution(mesh):
    held = P("section", "peer", None, None)
    return jax.shard_map(
        on_device,
        mesh=mesh,
        in_specs=(P("peer", None, "section"), P("peer", None, "section"), P("section", None)) + (held,) * 6 + (P(),),
        out_specs=(held,) * 6,
        check_vma=False,
    )
```
